32 devices in a mesh: groups: 2 (over x), ctx: 16 (over z, y, core).
Axes of the slice: x: 2, y: 2, z: 4, core: 2. Of those that a mesh axis runs over, the one named last changes fastest.
Arguments:
- query_input: bfloat16 [32, 1536], P('groups'), parts along dimension 0, may hold values from -20 to 20
- query_gain: bfloat16 [1536], replicated, may hold values from 0.5 to 1.5
- nope_weight: bfloat16 [1536, 4096], P(None, 'ctx'), may hold values from -0.15625 to 0.15625
- rope_weight: bfloat16 [1536, 2048], P(None, 'ctx'), may hold values from -0.15625 to 0.15625
- key_up: bfloat16 [32, 128, 512], P('ctx'), may hold values from -0.5 to 0.5
- value_up: bfloat16 [32, 512, 128], P('ctx'), may hold values from -1 to 1
- out_weight: bfloat16 [4096, 7168], P('ctx'), may hold values from -0.09375 to 0.09375
- cache_latent: bfloat16 [4, 32768, 512], P('groups', 'ctx'), parts along dimension 0, may hold values from -8 to 8
- cache_rope: bfloat16 [4, 64, 32768], P('groups', None, 'ctx'), parts along dimension 0, may hold values from -256 to 256
- cached_length: int32 [4], P('groups'), parts along dimension 0, may hold values from 16384 to 32760, as said below
Outputs:
- attn_out: bfloat16 [32, 7168], P('groups'), parts along dimension 0
The draws below stay inside these ranges and needn't reach their ends.
There are 2 independent parts, one for each index of `groups`. The reference program is written for one: setup_inputs(seed, part) draws one part's arguments, and reference() takes and returns one part's arrays. A program takes and returns all parts, laid end to end along the dimension named above; an argument that names none is the same for every part. Nothing has to cross between parts.
Inputs may be any that keep to these rules, and one draw needn't show every extreme that they name: `cached_length`: in every part one request has exactly 32760, so that its last new token sees the cache's last position.
All inputs are finite; a program needn't handle non-finite values.
Results may differ from the reference program's by a relative error of at most 0.012.
Values may be sent and summed in bfloat16 or wider, within the bound.
No kernel may reach another device: no remote copies, remote signals or barrier semaphores. Data moves between devices by JAX's collectives and lax.ppermute only.
A program may use at most 128 MiB of HBM per device.

```python
import math
import jax
import jax.numpy as jnp
from jax import lax

D = 7168
QR = 1536
NOPE = 128
ROPE = 64
LAT = 512
VDIM = 128
REQS = 2
STRETCH = 8
CTX_DEV = 2048
HEADS = 32
ROWS = 16
CACHE = 32768
N_CTX = 16


def key_scales(key, smallest, widest):
    spread = jax.random.uniform(jax.random.fold_in(key, 11), (REQS, CACHE), jnp.float32)
    return jnp.exp(jnp.log(smallest) + spread * jnp.log(widest))


def latent_region(key):
    mode_count = 2 * (CACHE // CTX_DEV)
    phases = jax.random.uniform(jax.random.fold_in(key, 13), (REQS, 1, mode_count), jnp.float32) * (2.0 * math.pi)
    vectors = jax.random.normal(jax.random.fold_in(key, 14), (REQS, mode_count, LAT), jnp.float32)
    frequency = (jnp.arange(mode_count, dtype=jnp.float32) + 1.0) * (math.pi / CACHE)
    position = jnp.arange(CACHE, dtype=jnp.float32)
    wave_table = jnp.cos(position[None, :, None] * frequency[None, None, :] + phases) * math.sqrt(2.0 / mode_count)
    return jnp.einsum('bpk,bkl->bpl', wave_table, vectors)


def draw_query_input(key, part):
    spread = jax.random.uniform(jax.random.fold_in(key, 41), (ROWS, 1), jnp.float32)
    row_scale = jnp.exp(jnp.log(0.3) + spread * jnp.log(10.0))
    entries = jax.random.normal(jax.random.fold_in(key, 42), (ROWS, QR), jnp.float32)
    return jnp.clip(entries * row_scale, -20.0, 20.0).astype(jnp.bfloat16)


def draw_cache_latent(key, part):
    scales = key_scales(key, 0.08, 5.0)
    entries = jax.random.normal(jax.random.fold_in(key, 21), (REQS, CACHE, LAT), jnp.float32)
    scaled = (entries + latent_region(key)) * scales[:, :, None]
    return jnp.clip(scaled, -8.0, 8.0).astype(jnp.bfloat16)


def draw_cache_rope(key, part):
    chosen = jax.random.randint(jax.random.fold_in(key, 32), (REQS, 8), 0, CACHE // 2)
    marked = jnp.any(jnp.arange(CACHE, dtype=jnp.int32)[None, None, :] == chosen[:, :, None], axis=1)
    sink_strength = 0.65 * math.log(CACHE)
    scales = key_scales(key, 0.08, 5.0)
    entries = jax.random.normal(jax.random.fold_in(key, 31), (REQS, ROPE, CACHE), jnp.float32)
    scaled = jnp.where(marked[:, None, :], entries * sink_strength, entries * scales[:, None, :])
    return jnp.clip(scaled, -256.0, 256.0).astype(jnp.bfloat16)


def draw_cached_length(key, part):
    longest = jax.random.randint(jax.random.fold_in(key, 51), (), 0, REQS)
    others = jax.random.randint(jax.random.fold_in(key, 52), (REQS,), CACHE // 2, CACHE - STRETCH + 1)
    return jnp.where(jnp.arange(REQS, dtype=jnp.int32) == longest, CACHE - STRETCH, others).astype(jnp.int32)


def block_scale(stream_key, extent, cuts, low, high):
    loudness, own = 1.0, jax.random.fold_in(stream_key, 6)
    for axis_at, blocks in cuts:
        heights = jnp.exp(jax.random.uniform(jax.random.fold_in(own, axis_at), (blocks,), jnp.float32, low / len(cuts), high / len(cuts)))
        loudness = loudness * jnp.repeat(heights, extent[axis_at] // blocks).reshape([-1 if axis == axis_at else 1 for axis in range(len(extent))])
    return loudness


def noise(key, extent, width, most, split=(), held_as=jnp.bfloat16):
    factor_of = block_scale(key, extent, split, -0.22, 0.18) if split else 1.0
    result = jax.random.normal(key, extent, jnp.float32) * width * factor_of
    return jnp.minimum(jnp.maximum(result, -most), most).astype(held_as)


def setup_inputs(seed: int = 0, part: int = 0) -> dict:
    splits = jax.random.split(jax.random.key(seed), 11)
    part_keys = jax.random.split(jax.random.fold_in(splits[10], part), 11)
    return {
        "query_input": draw_query_input(jax.random.fold_in(jax.random.fold_in(splits[10], part), 71), part),
        "query_gain": jnp.clip(1.0 + 0.1 * jax.random.normal(splits[1], (QR,), jnp.float32), 0.5, 1.5).astype(jnp.bfloat16),
        "nope_weight": noise(splits[2], (QR, HEADS * NOPE), QR ** -0.5, 0.15625, ((1, 16),)),
        "rope_weight": noise(splits[3], (QR, HEADS * ROPE), QR ** -0.5, 0.15625, ((1, 16),)),
        "key_up": noise(splits[4], (HEADS, NOPE, LAT), NOPE ** -0.5, 0.5, ((0, 16),)),
        "value_up": noise(splits[5], (HEADS, LAT, VDIM), (LAT // 16) ** -0.5, 1.0, ((0, 16),)),
        "out_weight": noise(splits[6], (HEADS * VDIM, D), (HEADS * VDIM) ** -0.5, 0.09375, ((0, 16),)),
        "cache_latent": draw_cache_latent(jax.random.fold_in(jax.random.fold_in(splits[10], part), 71), part),
        "cache_rope": draw_cache_rope(jax.random.fold_in(jax.random.fold_in(splits[10], part), 71), part),
        "cached_length": draw_cached_length(jax.random.fold_in(jax.random.fold_in(splits[10], part), 71), part),
    }


mscale_yarn = 1.0 + 0.1 * math.log(40.0)
masked_score = -1e+30

def reference(query_input, query_gain, nope_weight, rope_weight, key_up, value_up, out_weight, cache_latent, cache_rope, cached_length):
    widened = query_input.astype(jnp.float32)
    normed = (widened * lax.rsqrt(lax.optimization_barrier(jnp.mean(widened * widened, axis=-1, keepdims=True)) + 1e-06) * query_gain.astype(jnp.float32)).astype(jnp.bfloat16)
    query_nope = jnp.dot(normed, nope_weight, preferred_element_type=jnp.float32).astype(jnp.bfloat16).reshape(ROWS, HEADS, NOPE)
    query_rope = jnp.dot(normed, rope_weight, preferred_element_type=jnp.float32).astype(jnp.bfloat16).reshape(ROWS, HEADS, ROPE)
    query_latent = jnp.einsum('rhn,hnl->rhl', query_nope.astype(jnp.float32), key_up.astype(jnp.float32)).astype(jnp.bfloat16)
    softmax_scale = mscale_yarn * mscale_yarn / math.sqrt(NOPE + ROPE)
    latent_rows = query_latent.astype(jnp.float32).reshape(REQS, STRETCH, HEADS, LAT)
    rope_rows = query_rope.astype(jnp.float32).reshape(REQS, STRETCH, HEADS, ROPE)
    last_seen = cached_length.astype(jnp.int32)[:, None] + jnp.arange(STRETCH, dtype=jnp.int32)[None, :]

    def one_block(running, block):
        row_top, weight_sum, pooled = running
        first_key = (block * CTX_DEV).astype(jnp.int32)
        key_block = lax.dynamic_slice_in_dim(cache_latent, first_key, CTX_DEV, 1).astype(jnp.float32)
        rope_block = lax.dynamic_slice_in_dim(cache_rope, first_key, CTX_DEV, 2).astype(jnp.float32)
        positions = first_key + jnp.arange(CTX_DEV, dtype=jnp.int32)
        scores = softmax_scale * (jnp.einsum('bchl,bpl->bchp', latent_rows, key_block) + jnp.einsum('bche,bep->bchp', rope_rows, rope_block))
        visible = (positions[None, None, :] <= last_seen[:, :, None])[:, :, None, :]
        scores = jnp.where(visible, scores, masked_score)
        block_peak = lax.optimization_barrier(jnp.max(scores, axis=-1))
        weights = jnp.where(visible, jnp.exp(scores - block_peak[..., None]), 0.0)
        rounded = lax.optimization_barrier(weights.astype(jnp.bfloat16)).astype(jnp.float32)
        block_sum = lax.optimization_barrier(jnp.sum(weights, axis=-1))
        block_pool = jnp.einsum('bchp,bpl->bchl', rounded, key_block)
        new_top = jnp.maximum(row_top, block_peak)
        keep_old = jnp.exp(row_top - new_top)
        keep_new = jnp.exp(block_peak - new_top)
        weight_sum = weight_sum * keep_old + block_sum * keep_new
        pooled = pooled * keep_old[..., None] + block_pool * keep_new[..., None]
        return ((new_top, weight_sum, pooled), None)
    initial = (jnp.full((REQS, STRETCH, HEADS), masked_score, jnp.float32), jnp.zeros((REQS, STRETCH, HEADS), jnp.float32), jnp.zeros((REQS, STRETCH, HEADS, LAT), jnp.float32))
    finals, unused = lax.scan(one_block, initial, jnp.arange(N_CTX, dtype=jnp.int32))
    row_top, weight_sum, pooled = finals
    attended = (pooled / weight_sum[..., None]).astype(jnp.bfloat16).reshape(ROWS, HEADS, LAT)
    head_values = jnp.einsum('rhl,hlv->rhv', attended.astype(jnp.float32), value_up.astype(jnp.float32)).astype(jnp.bfloat16).reshape(ROWS, HEADS * VDIM)
    return jnp.dot(head_values, out_weight, preferred_element_type=jnp.float32).astype(jnp.bfloat16)
```

```python
import functools
import math

import jax
import jax.numpy as jnp
from jax import lax
from jax.experimental import pallas as pl
from jax.experimental.pallas import tpu as pltpu
from jax.sharding import PartitionSpec as P

mscale_yarn = 1.0 + 0.1 * math.log(40.0)
masked_score = -1e30
LOG2E = 1.4426950408889634
LANES = 128
F32 = jnp.float32
BF16 = jnp.bfloat16


def stage_list(count):
    stages, stride = [], 1
    while stride < count:
        left = count // stride
        radix = 2 if (stride < 4 or left < 4) else 4
        stages.append((stride, radix))
        stride *= radix
    return stages


def swap(x, count, mask):
    return lax.ppermute(x, "ctx", [(i, i ^ mask) for i in range(count)])


def call(body, outs, operands, *, flops=0, smem=(), name=None, limit=40 << 20):
    specs = [
        pl.BlockSpec(memory_space=pltpu.SMEM if i in smem else pltpu.VMEM)
        for i in range(len(operands))
    ]
    total = sum(o.size * o.dtype.itemsize for o in list(outs) + list(operands))
    return pl.pallas_call(
        body,
        out_shape=tuple(outs),
        in_specs=specs,
        out_specs=tuple(pl.BlockSpec(memory_space=pltpu.VMEM) for _ in outs),
        compiler_params=pltpu.CompilerParams(vmem_limit_bytes=limit),
        cost_estimate=pl.CostEstimate(flops=flops, bytes_accessed=total, transcendentals=0),
        name=name,
    )(*operands)


def spec(shape, dtype):
    return jax.ShapeDtypeStruct(shape, dtype)


def query_body(heads, reqs, x_ref, gain_ref, nope_ref, rope_ref, key_ref, out_ref):
    rows = x_ref.shape[0]
    stretch = rows // reqs
    nope_width, latent = key_ref.shape[1], key_ref.shape[2]
    rope_width = rope_ref.shape[1] // heads
    x = x_ref[...].astype(F32)
    mean = jnp.mean(x * x, axis=-1, keepdims=True)
    normed = (x * lax.rsqrt(mean + 1e-06) * gain_ref[...].astype(F32)).astype(BF16)
    nope = jnp.dot(normed, nope_ref[...], preferred_element_type=F32).astype(BF16)
    rope = jnp.dot(normed, rope_ref[...], preferred_element_type=F32)
    lat = [
        jnp.dot(
            nope[:, h * nope_width : (h + 1) * nope_width], key_ref[h], preferred_element_type=F32
        )
        for h in range(heads)
    ]
    ropes = []
    for b in range(reqs):
        part = slice(b * stretch, (b + 1) * stretch)
        rows_b = jnp.concatenate([lat[h][part] for h in range(heads)], axis=0)
        out_ref[:, b * latent : (b + 1) * latent] = rows_b.astype(BF16)
        ropes.append(
            jnp.concatenate(
                [rope[part, h * rope_width : (h + 1) * rope_width] for h in range(heads)], axis=0
            )
        )
    out_ref[:, reqs * latent :] = jnp.concatenate(ropes, axis=1).astype(BF16)


def pack_stats(columns):
    rows = columns[0].shape[0]
    lane = lax.broadcasted_iota(jnp.int32, (rows, LANES), 1)
    out = jnp.zeros((rows, LANES), F32)
    for b, column in enumerate(columns):
        high = column.astype(BF16).astype(F32)
        rest = column - high
        mid = rest.astype(BF16).astype(F32)
        low = rest - mid
        for k, term in enumerate((high, mid, low)):
            out = jnp.where(lane == 3 * b + k, term, out)
    return out


def read_stats(stats, b):
    return (stats[:, 3 * b : 3 * b + 1] + stats[:, 3 * b + 1 : 3 * b + 2]) + stats[
        :, 3 * b + 2 : 3 * b + 3
    ]


def merge(parts, reqs, latent):
    tops = []
    pooled = []
    for b in range(reqs):
        lse = [read_stats(p[:, reqs * latent :], b) for p in parts]
        top = functools.reduce(jnp.maximum, lse)
        weight = [jnp.exp(m - top) for m in lse]
        total = functools.reduce(jnp.add, weight)
        inverse = 1.0 / total
        value = functools.reduce(
            jnp.add,
            [p[:, b * latent : (b + 1) * latent] * (w * inverse) for p, w in zip(parts, weight)],
        )
        pooled.append(value)
        tops.append(top + jnp.log(total))
    return pooled, tops


def attend_body(
    n_q, reqs, latent, rope_width, stretch, scale, chunk, *refs
):
    length_ref, q_refs = refs[0], refs[1 : 1 + n_q]
    lat_ref, rope_ref = refs[1 + n_q], refs[2 + n_q]
    keep_ref, send_ref = refs[3 + n_q], refs[4 + n_q]
    q_s, s_s = refs[5 + n_q], refs[6 + n_q]
    rows = q_s.shape[0]
    half = rows // 2
    keys = lat_ref.shape[1]
    at = 0
    for q in q_refs:
        q_s[at : at + q.shape[0], :] = q[...]
        at += q.shape[0]
    first_key = lax.axis_index("ctx") * keys
    block = min(rows, 256)
    for r0 in range(0, rows, block):
        rs = slice(r0, r0 + block)
        stats = []
        for b in range(reqs):
            seen = (
                length_ref[b]
                - first_key
                + lax.broadcasted_iota(jnp.int32, (stretch, chunk), 0)
            )
            lane = lax.broadcasted_iota(jnp.int32, (stretch, chunk), 1)
            lhs = q_s[rs, b * latent : (b + 1) * latent]
            base = reqs * latent + b * rope_width
            lhs_rope = q_s[rs, base : base + rope_width]
            peak = None
            for k0 in range(0, keys, chunk):
                s = lax.dot_general(
                    lhs,
                    lat_ref[b, k0 : k0 + chunk, :],
                    (((1,), (1,)), ((), ())),
                    preferred_element_type=F32,
                ) + jnp.dot(
                    lhs_rope, rope_ref[b, :, k0 : k0 + chunk], preferred_element_type=F32
                )
                visible = (lane + k0) <= seen
                s = jnp.where(
                    visible[None], s.reshape(block // stretch, stretch, chunk), masked_score
                ).reshape(block, chunk)
                s_s[b, :, k0 : k0 + chunk] = s
                top = jnp.max(s, axis=1, keepdims=True)
                peak = top if peak is None else jnp.maximum(peak, top)
            total, pool = None, None
            for k0 in range(0, keys, chunk):
                w = jnp.exp2((s_s[b, :, k0 : k0 + chunk] - peak) * (scale * LOG2E))
                part = jnp.sum(w, axis=1, keepdims=True)
                term = jnp.dot(
                    w.astype(BF16), lat_ref[b, k0 : k0 + chunk, :], preferred_element_type=F32
                )
                total = part if total is None else total + part
                pool = term if pool is None else pool + term
            pool = pool * (1.0 / total)
            stats.append(peak * scale + jnp.log(total))
            cols = slice(b * latent, (b + 1) * latent)
            for lo in range(r0, r0 + block, min(block, half)):
                size = min(block, half)
                piece = pool[lo - r0 : lo - r0 + size]
                if lo < half:
                    keep_ref[lo : lo + size, cols] = piece
                else:
                    send_ref[lo - half : lo - half + size, cols] = piece.astype(BF16)
        packed = pack_stats(stats)
        for lo in range(r0, r0 + block, min(block, half)):
            size = min(block, half)
            piece = packed[lo - r0 : lo - r0 + size]
            if lo < half:
                keep_ref[lo : lo + size, reqs * latent :] = piece
            else:
                send_ref[lo - half : lo - half + size, reqs * latent :] = piece.astype(BF16)


def merge_body(n_in, reqs, latent, *refs):
    parts = [r[...].astype(F32) for r in refs[:n_in]]
    outs = refs[n_in:]
    pooled, tops = merge(parts, reqs, latent)
    packed = pack_stats(tops)
    size = outs[0].shape[0]
    for j, out in enumerate(outs):
        rows = slice(j * size, (j + 1) * size)
        for b in range(reqs):
            out[:, b * latent : (b + 1) * latent] = pooled[b][rows].astype(out.dtype)
        out[:, reqs * latent :] = packed[rows].astype(out.dtype)


def project_body(n_in, reqs, heads, latent, parts_out, *refs):
    parts = [r[...].astype(F32) for r in refs[:n_in]]
    value_ref, weight_ref = refs[n_in], refs[n_in + 1]
    keep_ref, send_ref = refs[n_in + 2], refs[n_in + 3]
    pooled, _ = merge(parts, reqs, latent)
    stretch = pooled[0].shape[0] // heads
    values = []
    for h in range(heads):
        rows = jnp.concatenate([p[h * stretch : (h + 1) * stretch] for p in pooled], axis=0)
        values.append(
            jnp.dot(rows.astype(BF16), value_ref[h], preferred_element_type=F32).astype(BF16)
        )
    hidden = jnp.concatenate(values, axis=1)
    mine = lax.rem(lax.axis_index("ctx"), parts_out)
    width = weight_ref.shape[1] // parts_out
    for e in range(parts_out):
        start = pl.multiple_of(jnp.bitwise_xor(mine, e) * width, LANES)
        out = jnp.dot(hidden, weight_ref[:, pl.ds(start, width)], preferred_element_type=F32)
        slot = slice((e // 2) * width, (e // 2 + 1) * width)
        if e % 2 == 0:
            keep_ref[:, slot] = out
        else:
            send_ref[:, slot] = out.astype(BF16)


def place_body(parts_out, *refs):
    pieces, out_ref = refs[:-1], refs[-1]
    mine = lax.rem(lax.axis_index("ctx"), parts_out)
    width = out_ref.shape[1] // parts_out
    e_order = (0, 2, 1, 3)
    at = 0
    for piece in pieces:
        for k in range(piece.shape[1] // width):
            start = pl.multiple_of(jnp.bitwise_xor(mine, e_order[at]) * width, LANES)
            out_ref[:, pl.ds(start, width)] = piece[:, k * width : (k + 1) * width]
            at += 1


def local(count, query_input, query_gain, nope_weight, rope_weight, key_up, value_up, out_weight,
          cache_latent, cache_rope, cached_length):
    heads, nope_width, latent = key_up.shape
    reqs = cache_latent.shape[0]
    rope_width = cache_rope.shape[1]
    rows = query_input.shape[0]
    stretch = rows // reqs
    own = heads * stretch
    width = reqs * latent + LANES
    stages = stage_list(count)
    scale = mscale_yarn * mscale_yarn / math.sqrt(nope_width + rope_width)

    (query,) = call(
        functools.partial(query_body, heads, reqs),
        [spec((own, width), BF16)],
        [query_input, query_gain[None], nope_weight, rope_weight, key_up],
        name="query",
    )
    held = query
    for stride, radix in reversed(stages[2:]):
        got = [swap(held, count, j * stride) for j in range(1, radix)]
        held = jnp.concatenate([held] + got, axis=0)
    beside = swap(held, count, stages[1][0])
    near = jnp.concatenate([held, beside], axis=0)
    far = swap(near, count, stages[0][0])

    half = near.shape[0]
    total = 2 * half
    block = min(total, 256)
    operands = [cached_length, near, far, cache_latent, cache_rope]
    keep, send = pl.pallas_call(
        functools.partial(attend_body, 2, reqs, latent, rope_width, stretch, scale, 512),
        out_shape=(spec((half, width), F32), spec((half, width), BF16)),
        in_specs=[pl.BlockSpec(memory_space=pltpu.SMEM)]
        + [pl.BlockSpec(memory_space=pltpu.VMEM)] * 4,
        out_specs=(pl.BlockSpec(memory_space=pltpu.VMEM),) * 2,
        scratch_shapes=[
            pltpu.VMEM((total, width), BF16),
            pltpu.VMEM((reqs, block, cache_latent.shape[1]), F32),
        ],
        compiler_params=pltpu.CompilerParams(vmem_limit_bytes=48 << 20),
        cost_estimate=pl.CostEstimate(
            flops=4 * total * cache_latent.shape[1] * latent * reqs,
            bytes_accessed=8 << 20,
            transcendentals=0,
        ),
        name="attend",
    )(*operands)

    got = [swap(send, count, stages[0][0])]
    for stride, radix in stages[1:]:
        size = keep.shape[0] // radix
        pieces = call(
            functools.partial(merge_body, 1 + len(got), reqs, latent),
            [spec((size, width), F32)] + [spec((size, width), BF16)] * (radix - 1),
            [keep] + got,
            name="merge",
        )
        keep = pieces[0]
        got = [swap(p, count, j * stride) for j, p in enumerate(pieces[1:], 1)]

    parts_out = 4
    model = out_weight.shape[1]
    quarter = model // parts_out
    keep, send = call(
        functools.partial(project_body, 1 + len(got), reqs, heads, latent, parts_out),
        [spec((rows, 2 * quarter), F32), spec((rows, 2 * quarter), BF16)],
        [keep] + got + [value_up, out_weight],
        name="project",
    )
    kept = keep + swap(send, count, stages[0][0]).astype(F32)
    kept = kept[:, :quarter] + swap(kept[:, quarter:].astype(BF16), count, stages[1][0]).astype(F32)
    for stride, radix in stages[2:]:
        mine = kept.astype(BF16)
        terms = [mine.astype(F32)] + [
            swap(mine, count, j * stride).astype(F32) for j in range(1, radix)
        ]
        while len(terms) > 1:
            terms = [terms[i] + terms[i + 1] for i in range(0, len(terms), 2)]
        kept = terms[0]
    done = kept.astype(BF16)
    both = jnp.concatenate([done, swap(done, count, stages[1][0])], axis=1)
    other = swap(both, count, stages[0][0])
    (out,) = call(
        functools.partial(place_body, parts_out),
        [spec((rows, model), BF16)],
        [both, other],
        name="place",
    )
    return out


def solution(mesh):
    placed = (
        P("groups", None),
        P(),
        P(None, "ctx"),
        P(None, "ctx"),
        P("ctx", None, None),
        P("ctx", None, None),
        P("ctx", None),
        P("groups", "ctx", None),
        P("groups", None, "ctx"),
        P("groups"),
    )
    return jax.shard_map(
        functools.partial(local, mesh.shape["ctx"]),
        mesh=mesh,
        in_specs=placed,
        out_specs=P("groups", None),
        check_vma=False,
    )
```

```python
import functools
import math

import jax
import jax.numpy as jnp
from jax import lax
from jax.experimental import pallas as pl
from jax.experimental.pallas import tpu as pltpu
from jax.sharding import PartitionSpec as P

mscale_yarn = 1.0 + 0.1 * math.log(40.0)
masked_score = -1e30
LOG2E = 1.4426950408889634
LANES = 128
F32 = jnp.float32
BF16 = jnp.bfloat16


def stage_list(count):
    stages, stride = [], 1
    while stride < count:
        left = count // stride
        radix = 2 if (stride < 4 or left < 4) else 4
        stages.append((stride, radix))
        stride *= radix
    return stages


def swap(x, count, mask):
    return lax.ppermute(x, "ctx", [(i, i ^ mask) for i in range(count)])


def call(body, outs, operands, *, flops=0, smem=(), name=None, limit=40 << 20):
    specs = [
        pl.BlockSpec(memory_space=pltpu.SMEM if i in smem else pltpu.VMEM)
        for i in range(len(operands))
    ]
    total = sum(o.size * o.dtype.itemsize for o in list(outs) + list(operands))
    return pl.pallas_call(
        body,
        out_shape=tuple(outs),
        in_specs=specs,
        out_specs=tuple(pl.BlockSpec(memory_space=pltpu.VMEM) for _ in outs),
        compiler_params=pltpu.CompilerParams(vmem_limit_bytes=limit),
        cost_estimate=pl.CostEstimate(flops=flops, bytes_accessed=total, transcendentals=0),
        name=name,
    )(*operands)


def spec(shape, dtype):
    return jax.ShapeDtypeStruct(shape, dtype)


def query_body(heads, reqs, *refs):
    sources, out_ref, (x_ref, gain_ref, nope_ref, rope_ref, key_ref), sems = (
        refs[:5], refs[5], refs[6:11], refs[11]
    )
    copies = [
        pltpu.make_async_copy(source, held, sems.at[i])
        for i, (source, held) in enumerate(zip(sources, refs[6:11]))
    ]
    for copy in copies:
        copy.start()
    rows = x_ref.shape[0]
    stretch = rows // reqs
    nope_width, latent = key_ref.shape[1], key_ref.shape[2]
    rope_width = rope_ref.shape[1] // heads
    copies[0].wait()
    copies[1].wait()
    x = x_ref[...].astype(F32)
    mean = jnp.mean(x * x, axis=-1, keepdims=True)
    gain = gain_ref[...].astype(F32).reshape(1, -1)
    normed = (x * lax.rsqrt(mean + 1e-06) * gain).astype(BF16)
    copies[2].wait()
    nope = jnp.dot(normed, nope_ref[...], preferred_element_type=F32).astype(BF16)
    copies[3].wait()
    rope = jnp.dot(normed, rope_ref[...], preferred_element_type=F32)
    copies[4].wait()
    lat = [
        jnp.dot(
            nope[:, h * nope_width : (h + 1) * nope_width], key_ref[h], preferred_element_type=F32
        )
        for h in range(heads)
    ]
    ropes = []
    for b in range(reqs):
        part = slice(b * stretch, (b + 1) * stretch)
        rows_b = jnp.concatenate([lat[h][part] for h in range(heads)], axis=0)
        out_ref[:, b * latent : (b + 1) * latent] = rows_b.astype(BF16)
        ropes.append(
            jnp.concatenate(
                [rope[part, h * rope_width : (h + 1) * rope_width] for h in range(heads)], axis=0
            )
        )
    out_ref[:, reqs * latent :] = jnp.concatenate(ropes, axis=1).astype(BF16)


def pack_stats(columns):
    rows = columns[0].shape[0]
    lane = lax.broadcasted_iota(jnp.int32, (rows, LANES), 1)
    out = jnp.zeros((rows, LANES), F32)
    for b, column in enumerate(columns):
        high = column.astype(BF16).astype(F32)
        rest = column - high
        mid = rest.astype(BF16).astype(F32)
        low = rest - mid
        for k, term in enumerate((high, mid, low)):
            out = jnp.where(lane == 3 * b + k, term, out)
    return out


def read_stats(stats, b):
    return (stats[:, 3 * b : 3 * b + 1] + stats[:, 3 * b + 1 : 3 * b + 2]) + stats[
        :, 3 * b + 2 : 3 * b + 3
    ]


def merge(parts, reqs, latent):
    tops = []
    pooled = []
    for b in range(reqs):
        lse = [read_stats(p[:, reqs * latent :], b) for p in parts]
        top = functools.reduce(jnp.maximum, lse)
        weight = [jnp.exp(m - top) for m in lse]
        total = functools.reduce(jnp.add, weight)
        inverse = 1.0 / total
        value = functools.reduce(
            jnp.add,
            [p[:, b * latent : (b + 1) * latent] * (w * inverse) for p, w in zip(parts, weight)],
        )
        pooled.append(value)
        tops.append(top + jnp.log(total))
    return pooled, tops


def attend_body(
    n_q, reqs, latent, rope_width, stretch, scale, chunk, *refs
):
    length_ref, q_refs = refs[0], refs[1 : 1 + n_q]
    lat_ref, rope_ref = refs[1 + n_q], refs[2 + n_q]
    keep_ref, send_ref = refs[3 + n_q], refs[4 + n_q]
    q_s, s_s = refs[5 + n_q], refs[6 + n_q]
    rows = q_s.shape[0]
    half = rows // 2
    keys = lat_ref.shape[1]
    at = 0
    for q in q_refs:
        q_s[at : at + q.shape[0], :] = q[...]
        at += q.shape[0]
    first_key = lax.axis_index("ctx") * keys
    block = min(rows, 256)
    for r0 in range(0, rows, block):
        rs = slice(r0, r0 + block)
        stats = []
        for b in range(reqs):
            seen = (
                length_ref[b]
                - first_key
                + lax.broadcasted_iota(jnp.int32, (stretch, chunk), 0)
            )
            lane = lax.broadcasted_iota(jnp.int32, (stretch, chunk), 1)
            lhs = q_s[rs, b * latent : (b + 1) * latent]
            base = reqs * latent + b * rope_width
            lhs_rope = q_s[rs, base : base + rope_width]
            peak = None
            for k0 in range(0, keys, chunk):
                s = lax.dot_general(
                    lhs,
                    lat_ref[b, k0 : k0 + chunk, :],
                    (((1,), (1,)), ((), ())),
                    preferred_element_type=F32,
                ) + jnp.dot(
                    lhs_rope, rope_ref[b, :, k0 : k0 + chunk], preferred_element_type=F32
                )
                visible = (lane + k0) <= seen
                s = jnp.where(
                    visible[None], s.reshape(block // stretch, stretch, chunk), masked_score
                ).reshape(block, chunk)
                s_s[b, :, k0 : k0 + chunk] = s
                top = jnp.max(s, axis=1, keepdims=True)
                peak = top if peak is None else jnp.maximum(peak, top)
            total, pool = None, None
            for k0 in range(0, keys, chunk):
                w = jnp.exp2((s_s[b, :, k0 : k0 + chunk] - peak) * (scale * LOG2E))
                part = jnp.sum(w, axis=1, keepdims=True)
                term = jnp.dot(
                    w.astype(BF16), lat_ref[b, k0 : k0 + chunk, :], preferred_element_type=F32
                )
                total = part if total is None else total + part
                pool = term if pool is None else pool + term
            pool = pool * (1.0 / total)
            stats.append(peak * scale + jnp.log(total))
            cols = slice(b * latent, (b + 1) * latent)
            for lo in range(r0, r0 + block, min(block, half)):
                size = min(block, half)
                piece = pool[lo - r0 : lo - r0 + size]
                if lo < half:
                    keep_ref[lo : lo + size, cols] = piece
                else:
                    send_ref[lo - half : lo - half + size, cols] = piece.astype(BF16)
        packed = pack_stats(stats)
        for lo in range(r0, r0 + block, min(block, half)):
            size = min(block, half)
            piece = packed[lo - r0 : lo - r0 + size]
            if lo < half:
                keep_ref[lo : lo + size, reqs * latent :] = piece
            else:
                send_ref[lo - half : lo - half + size, reqs * latent :] = piece.astype(BF16)


def merge_body(n_in, reqs, latent, *refs):
    parts = [r[...].astype(F32) for r in refs[:n_in]]
    outs = refs[n_in:]
    pooled, tops = merge(parts, reqs, latent)
    packed = pack_stats(tops)
    size = outs[0].shape[0]
    for j, out in enumerate(outs):
        rows = slice(j * size, (j + 1) * size)
        for b in range(reqs):
            out[:, b * latent : (b + 1) * latent] = pooled[b][rows].astype(out.dtype)
        out[:, reqs * latent :] = packed[rows].astype(out.dtype)


def project_body(n_in, reqs, heads, latent, parts_out, *refs):
    parts = [r[...].astype(F32) for r in refs[:n_in]]
    value_ref, weight_ref = refs[n_in], refs[n_in + 1]
    keep_ref, send_ref = refs[n_in + 2], refs[n_in + 3]
    pooled, _ = merge(parts, reqs, latent)
    stretch = pooled[0].shape[0] // heads
    values = []
    for h in range(heads):
        rows = jnp.concatenate([p[h * stretch : (h + 1) * stretch] for p in pooled], axis=0)
        values.append(
            jnp.dot(rows.astype(BF16), value_ref[h], preferred_element_type=F32).astype(BF16)
        )
    hidden = jnp.concatenate(values, axis=1)
    mine = lax.rem(lax.axis_index("ctx"), parts_out)
    width = weight_ref.shape[1] // parts_out
    for e in range(parts_out):
        start = pl.multiple_of(jnp.bitwise_xor(mine, e) * width, LANES)
        out = jnp.dot(hidden, weight_ref[:, pl.ds(start, width)], preferred_element_type=F32)
        slot = slice((e // 2) * width, (e // 2 + 1) * width)
        if e % 2 == 0:
            keep_ref[:, slot] = out
        else:
            send_ref[:, slot] = out.astype(BF16)


def join_body(*refs):
    at = 0
    for r in refs[:-1]:
        refs[-1][at : at + r.shape[0], :] = r[...]
        at += r.shape[0]


def place_body(parts_out, *refs):
    pieces, out_ref, sems = refs[:-2], refs[-2], refs[-1]
    copies = []
    mine = lax.rem(lax.axis_index("ctx"), parts_out)
    width = out_ref.shape[1] // parts_out
    e_order = (0, 2, 1, 3)
    at = 0
    for piece in pieces:
        for k in range(piece.shape[1] // width):
            start = pl.multiple_of(jnp.bitwise_xor(mine, e_order[at]) * width, LANES)
            copies.append(
                pltpu.make_async_copy(
                    piece.at[:, pl.ds(k * width, width)],
                    out_ref.at[:, pl.ds(start, width)],
                    sems.at[at],
                )
            )
            copies[-1].start()
            at += 1
    for copy in copies:
        copy.wait()


def local(count, query_input, query_gain, nope_weight, rope_weight, key_up, value_up, out_weight,
          cache_latent, cache_rope, cached_length):
    heads, nope_width, latent = key_up.shape
    reqs = cache_latent.shape[0]
    rope_width = cache_rope.shape[1]
    rows = query_input.shape[0]
    stretch = rows // reqs
    own = heads * stretch
    width = reqs * latent + LANES
    stages = stage_list(count)
    scale = mscale_yarn * mscale_yarn / math.sqrt(nope_width + rope_width)

    sources = [query_input, query_gain, nope_weight, rope_weight, key_up]
    query = pl.pallas_call(
        functools.partial(query_body, heads, reqs),
        out_shape=spec((own, width), BF16),
        in_specs=[pl.BlockSpec(memory_space=pl.ANY)] * len(sources),
        out_specs=pl.BlockSpec(memory_space=pltpu.VMEM),
        scratch_shapes=[pltpu.VMEM(a.shape, a.dtype) for a in sources]
        + [pltpu.SemaphoreType.DMA((len(sources),))],
        compiler_params=pltpu.CompilerParams(vmem_limit_bytes=24 << 20),
        cost_estimate=pl.CostEstimate(flops=1 << 24, bytes_accessed=1 << 21, transcendentals=0),
        name="query",
    )(*sources)
    join_flops = 4 << 30
    held = query
    for stride, radix in reversed(stages[2:]):
        got = [swap(held, count, j * stride) for j in range(1, radix)]
        parts = [held] + got
        (held,) = call(
            join_body,
            [spec((radix * held.shape[0], width), BF16)],
            parts,
            flops=join_flops,
            limit=16 << 20,
            name="join",
        )
    beside = swap(held, count, stages[1][0])
    near = jnp.concatenate([held, beside], axis=0)
    far = swap(near, count, stages[0][0])

    half = near.shape[0]
    total = 2 * half
    block = min(total, 256)
    operands = [cached_length, near, far, cache_latent, cache_rope]
    keep, send = pl.pallas_call(
        functools.partial(attend_body, 2, reqs, latent, rope_width, stretch, scale, 512),
        out_shape=(spec((half, width), F32), spec((half, width), BF16)),
        in_specs=[pl.BlockSpec(memory_space=pltpu.SMEM)]
        + [pl.BlockSpec(memory_space=pltpu.VMEM)] * 4,
        out_specs=(pl.BlockSpec(memory_space=pltpu.VMEM),) * 2,
        scratch_shapes=[
            pltpu.VMEM((total, width), BF16),
            pltpu.VMEM((reqs, block, cache_latent.shape[1]), F32),
        ],
        compiler_params=pltpu.CompilerParams(vmem_limit_bytes=48 << 20),
        cost_estimate=pl.CostEstimate(
            flops=4 * total * cache_latent.shape[1] * latent * reqs,
            bytes_accessed=8 << 20,
            transcendentals=0,
        ),
        name="attend",
    )(*operands)

    got = [swap(send, count, stages[0][0])]
    for stride, radix in stages[1:]:
        size = keep.shape[0] // radix
        pieces = call(
            functools.partial(merge_body, 1 + len(got), reqs, latent),
            [spec((size, width), F32)] + [spec((size, width), BF16)] * (radix - 1),
            [keep] + got,
            name="merge",
        )
        keep = pieces[0]
        got = [swap(pieces[j], count, j * stride) for j in reversed(range(1, radix))]

    parts_out = 4
    model = out_weight.shape[1]
    quarter = model // parts_out
    keep, send = call(
        functools.partial(project_body, 1 + len(got), reqs, heads, latent, parts_out),
        [spec((rows, 2 * quarter), F32), spec((rows, 2 * quarter), BF16)],
        [keep] + got + [value_up, out_weight],
        name="project",
    )
    kept = keep + swap(send, count, stages[0][0]).astype(F32)
    kept = kept[:, :quarter] + swap(kept[:, quarter:].astype(BF16), count, stages[1][0]).astype(F32)
    for stride, radix in stages[2:]:
        mine = kept.astype(BF16)
        terms = [mine.astype(F32)] + [
            swap(mine, count, j * stride).astype(F32) for j in range(1, radix)
        ]
        while len(terms) > 1:
            terms = [terms[i] + terms[i + 1] for i in range(0, len(terms), 2)]
        kept = terms[0]
    done = kept.astype(BF16)
    both = jnp.concatenate([done, swap(done, count, stages[1][0])], axis=1)
    other = swap(both, count, stages[0][0])
    return pl.pallas_call(
        functools.partial(place_body, parts_out),
        out_shape=spec((rows, model), BF16),
        in_specs=[pl.BlockSpec(memory_space=pltpu.VMEM)] * 2,
        out_specs=pl.BlockSpec(memory_space=pl.ANY),
        scratch_shapes=[pltpu.SemaphoreType.DMA((parts_out,))],
        compiler_params=pltpu.CompilerParams(vmem_limit_bytes=16 << 20),
        name="place",
    )(both, other)


def solution(mesh):
    placed = (
        P("groups", None),
        P(),
        P(None, "ctx"),
        P(None, "ctx"),
        P("ctx", None, None),
        P("ctx", None, None),
        P("ctx", None),
        P("groups", "ctx", None),
        P("groups", None, "ctx"),
        P("groups"),
    )
    return jax.shard_map(
        functools.partial(local, mesh.shape["ctx"]),
        mesh=mesh,
        in_specs=placed,
        out_specs=P("groups", None),
        check_vma=False,
    )
```

```python
import functools
import math

import jax
import jax.numpy as jnp
from jax import lax
from jax.experimental import pallas as pl
from jax.experimental.pallas import tpu as pltpu
from jax.sharding import PartitionSpec as P

mscale_yarn = 1.0 + 0.1 * math.log(40.0)
masked_score = -1e30
LOG2E = 1.4426950408889634
LANES = 128
F32 = jnp.float32
BF16 = jnp.bfloat16


def stage_list(count):
    stages, stride = [], 1
    while stride < count:
        left = count // stride
        radix = 2 if (stride < 4 or left < 4) else 4
        stages.append((stride, radix))
        stride *= radix
    return stages


def swap(x, count, mask):
    return lax.ppermute(x, "ctx", [(i, i ^ mask) for i in range(count)])


def call(body, outs, operands, *, flops=0, smem=(), name=None, limit=40 << 20):
    specs = [
        pl.BlockSpec(memory_space=pltpu.SMEM if i in smem else pltpu.VMEM)
        for i in range(len(operands))
    ]
    total = sum(o.size * o.dtype.itemsize for o in list(outs) + list(operands))
    return pl.pallas_call(
        body,
        out_shape=tuple(outs),
        in_specs=specs,
        out_specs=tuple(pl.BlockSpec(memory_space=pltpu.VMEM) for _ in outs),
        compiler_params=pltpu.CompilerParams(vmem_limit_bytes=limit),
        cost_estimate=pl.CostEstimate(flops=flops, bytes_accessed=total, transcendentals=0),
        name=name,
    )(*operands)


def spec(shape, dtype):
    return jax.ShapeDtypeStruct(shape, dtype)


def table_body(keys, table_ref):
    table_ref[...] = (
        lax.axis_index("ctx") * keys
        + lax.broadcasted_iota(jnp.int32, table_ref.shape, 1)
        - lax.broadcasted_iota(jnp.int32, table_ref.shape, 0)
    )


def query_body(heads, reqs, x_ref, gain_ref, nope_ref, rope_ref, key_ref, table_ref, out_ref):
    rows = x_ref.shape[0]
    stretch = rows // reqs
    nope_width, latent = key_ref.shape[1], key_ref.shape[2]
    rope_width = rope_ref.shape[1] // heads
    x = x_ref[...].astype(F32)
    mean = jnp.mean(x * x, axis=-1, keepdims=True)
    normed = (x * lax.rsqrt(mean + 1e-06) * gain_ref[...].astype(F32).reshape(1, -1)).astype(BF16)
    nope = jnp.dot(normed, nope_ref[...], preferred_element_type=F32).astype(BF16)
    rope = jnp.dot(normed, rope_ref[...], preferred_element_type=F32)
    lat = [
        jnp.dot(
            nope[:, h * nope_width : (h + 1) * nope_width], key_ref[h], preferred_element_type=F32
        )
        for h in range(heads)
    ]
    ropes = []
    for b in range(reqs):
        part = slice(b * stretch, (b + 1) * stretch)
        rows_b = jnp.concatenate([lat[h][part] for h in range(heads)], axis=0)
        out_ref[:, b * latent : (b + 1) * latent] = rows_b.astype(BF16)
        ropes.append(
            jnp.concatenate(
                [rope[part, h * rope_width : (h + 1) * rope_width] for h in range(heads)], axis=0
            )
        )
    out_ref[:, reqs * latent :] = jnp.concatenate(ropes, axis=1).astype(BF16)


def pack_stats(columns):
    rows = columns[0].shape[0]
    lane = lax.broadcasted_iota(jnp.int32, (rows, LANES), 1)
    out = jnp.zeros((rows, LANES), F32)
    for b, column in enumerate(columns):
        high = column.astype(BF16).astype(F32)
        rest = column - high
        mid = rest.astype(BF16).astype(F32)
        low = rest - mid
        for k, term in enumerate((high, mid, low)):
            out = jnp.where(lane == 3 * b + k, term, out)
    return out


def read_stats(stats, b):
    return (stats[:, 3 * b : 3 * b + 1] + stats[:, 3 * b + 1 : 3 * b + 2]) + stats[
        :, 3 * b + 2 : 3 * b + 3
    ]


def merge(parts, reqs, latent):
    tops = []
    pooled = []
    for b in range(reqs):
        lse = [read_stats(p[:, reqs * latent :], b) for p in parts]
        top = functools.reduce(jnp.maximum, lse)
        weight = [jnp.exp(m - top) for m in lse]
        total = functools.reduce(jnp.add, weight)
        inverse = 1.0 / total
        value = functools.reduce(
            jnp.add,
            [p[:, b * latent : (b + 1) * latent] * (w * inverse) for p, w in zip(parts, weight)],
        )
        pooled.append(value)
        tops.append(top + jnp.log(total))
    return pooled, tops


def attend_body(
    n_q, reqs, latent, rope_width, stretch, scale, chunk, *refs
):
    length_ref, table_ref, refs = refs[0], refs[1], refs[2:]
    q_refs = refs[:n_q]
    lat_ref, rope_ref = refs[n_q], refs[1 + n_q]
    keep_ref, send_ref = refs[2 + n_q], refs[3 + n_q]
    q_s, s_s = refs[4 + n_q], refs[5 + n_q]
    rows = q_s.shape[0]
    half = rows // 2
    keys = lat_ref.shape[1]
    at = 0
    for q in q_refs:
        q_s[at : at + q.shape[0], :] = q[...]
        at += q.shape[0]
    block = min(rows, 256)
    for r0 in range(0, rows, block):
        rs = slice(r0, r0 + block)
        stats = []
        for b in range(reqs):
            seen = length_ref[b]
            lhs = q_s[rs, b * latent : (b + 1) * latent]
            base = reqs * latent + b * rope_width
            lhs_rope = q_s[rs, base : base + rope_width]
            peak = None
            for k0 in range(0, keys, chunk):
                s = lax.dot_general(
                    lhs,
                    lat_ref[b, k0 : k0 + chunk, :],
                    (((1,), (1,)), ((), ())),
                    preferred_element_type=F32,
                ) + jnp.dot(
                    lhs_rope, rope_ref[b, :, k0 : k0 + chunk], preferred_element_type=F32
                )
                visible = table_ref[...] + k0 <= seen
                s = jnp.where(
                    visible[None], s.reshape(block // stretch, stretch, chunk), masked_score
                ).reshape(block, chunk)
                s_s[b, :, k0 : k0 + chunk] = s
                top = jnp.max(s, axis=1, keepdims=True)
                peak = top if peak is None else jnp.maximum(peak, top)
            total, pool = None, None
            for k0 in range(0, keys, chunk):
                w = jnp.exp2((s_s[b, :, k0 : k0 + chunk] - peak) * (scale * LOG2E))
                part = jnp.sum(w, axis=1, keepdims=True)
                term = jnp.dot(
                    w.astype(BF16), lat_ref[b, k0 : k0 + chunk, :], preferred_element_type=F32
                )
                total = part if total is None else total + part
                pool = term if pool is None else pool + term
            pool = pool * (1.0 / total)
            stats.append(peak * scale + jnp.log(total))
            cols = slice(b * latent, (b + 1) * latent)
            for lo in range(r0, r0 + block, min(block, half)):
                size = min(block, half)
                piece = pool[lo - r0 : lo - r0 + size]
                if lo < half:
                    keep_ref[lo : lo + size, cols] = piece
                else:
                    send_ref[lo - half : lo - half + size, cols] = piece.astype(BF16)
        packed = pack_stats(stats)
        for lo in range(r0, r0 + block, min(block, half)):
            size = min(block, half)
            piece = packed[lo - r0 : lo - r0 + size]
            if lo < half:
                keep_ref[lo : lo + size, reqs * latent :] = piece
            else:
                send_ref[lo - half : lo - half + size, reqs * latent :] = piece.astype(BF16)


def merge_body(n_in, reqs, latent, *refs):
    parts = [r[...].astype(F32) for r in refs[:n_in]]
    outs = refs[n_in:]
    pooled, tops = merge(parts, reqs, latent)
    packed = pack_stats(tops)
    size = outs[0].shape[0]
    for j, out in enumerate(outs):
        rows = slice(j * size, (j + 1) * size)
        for b in range(reqs):
            out[:, b * latent : (b + 1) * latent] = pooled[b][rows].astype(out.dtype)
        out[:, reqs * latent :] = packed[rows].astype(out.dtype)


def project_body(n_in, reqs, heads, latent, parts_out, *refs):
    parts = [r[...].astype(F32) for r in refs[:n_in]]
    value_ref, weight_ref = refs[n_in], refs[n_in + 1]
    keep_ref, send_ref = refs[n_in + 2], refs[n_in + 3]
    pooled, _ = merge(parts, reqs, latent)
    stretch = pooled[0].shape[0] // heads
    values = []
    for h in range(heads):
        rows = jnp.concatenate([p[h * stretch : (h + 1) * stretch] for p in pooled], axis=0)
        values.append(
            jnp.dot(rows.astype(BF16), value_ref[h], preferred_element_type=F32).astype(BF16)
        )
    hidden = jnp.concatenate(values, axis=1)
    mine = lax.rem(lax.axis_index("ctx"), parts_out)
    width = weight_ref.shape[1] // parts_out
    for e in range(parts_out):
        start = pl.multiple_of(jnp.bitwise_xor(mine, e) * width, LANES)
        out = jnp.dot(hidden, weight_ref[:, pl.ds(start, width)], preferred_element_type=F32)
        slot = slice((e // 2) * width, (e // 2 + 1) * width)
        if e % 2 == 0:
            keep_ref[:, slot] = out
        else:
            send_ref[:, slot] = out.astype(BF16)


def join_body(*refs):
    at = 0
    for r in refs[:-1]:
        refs[-1][at : at + r.shape[0], :] = r[...]
        at += r.shape[0]


def place_body(parts_out, *refs):
    pieces, out_ref, sems = refs[:-2], refs[-2], refs[-1]
    copies = []
    mine = lax.rem(lax.axis_index("ctx"), parts_out)
    width = out_ref.shape[1] // parts_out
    e_order = (0, 2, 1, 3)
    at = 0
    for piece in pieces:
        for k in range(piece.shape[1] // width):
            start = pl.multiple_of(jnp.bitwise_xor(mine, e_order[at]) * width, LANES)
            copies.append(
                pltpu.make_async_copy(
                    piece.at[:, pl.ds(k * width, width)],
                    out_ref.at[:, pl.ds(start, width)],
                    sems.at[at],
                )
            )
            copies[-1].start()
            at += 1
    for copy in copies:
        copy.wait()


def local(count, query_input, query_gain, nope_weight, rope_weight, key_up, value_up, out_weight,
          cache_latent, cache_rope, cached_length):
    heads, nope_width, latent = key_up.shape
    reqs = cache_latent.shape[0]
    rope_width = cache_rope.shape[1]
    rows = query_input.shape[0]
    stretch = rows // reqs
    own = heads * stretch
    width = reqs * latent + LANES
    stages = stage_list(count)
    scale = mscale_yarn * mscale_yarn / math.sqrt(nope_width + rope_width)

    chunk = 512
    (table,) = call(
        functools.partial(table_body, cache_latent.shape[1]),
        [spec((stretch, chunk), jnp.int32)],
        [],
        flops=2 << 30,
        limit=16 << 20,
        name="table",
    )
    (query,) = call(
        functools.partial(query_body, heads, reqs),
        [spec((own, width), BF16)],
        [query_input, query_gain, nope_weight, rope_weight, key_up, table],
        limit=16 << 20,
        name="query",
    )
    join_flops = 4 << 30
    held = query
    for stride, radix in reversed(stages[2:]):
        got = [swap(held, count, j * stride) for j in range(1, radix)]
        parts = [held] + got
        (held,) = call(
            join_body,
            [spec((radix * held.shape[0], width), BF16)],
            parts,
            flops=join_flops,
            limit=16 << 20,
            name="join",
        )
    beside = swap(held, count, stages[1][0])
    near = jnp.concatenate([held, beside], axis=0)
    far = swap(near, count, stages[0][0])

    half = near.shape[0]
    total = 2 * half
    block = min(total, 256)
    operands = [cached_length, table, near, far, cache_latent, cache_rope]
    keep, send = pl.pallas_call(
        functools.partial(attend_body, 2, reqs, latent, rope_width, stretch, scale, chunk),
        out_shape=(spec((half, width), F32), spec((half, width), BF16)),
        in_specs=[pl.BlockSpec(memory_space=pltpu.SMEM)]
        + [pl.BlockSpec(memory_space=pltpu.VMEM)] * 5,
        out_specs=(pl.BlockSpec(memory_space=pltpu.VMEM),) * 2,
        scratch_shapes=[
            pltpu.VMEM((total, width), BF16),
            pltpu.VMEM((reqs, block, cache_latent.shape[1]), F32),
        ],
        compiler_params=pltpu.CompilerParams(vmem_limit_bytes=48 << 20),
        cost_estimate=pl.CostEstimate(
            flops=4 * total * cache_latent.shape[1] * latent * reqs,
            bytes_accessed=8 << 20,
            transcendentals=0,
        ),
        name="attend",
    )(*operands)

    got = [swap(send, count, stages[0][0])]
    for stride, radix in stages[1:]:
        size = keep.shape[0] // radix
        pieces = call(
            functools.partial(merge_body, 1 + len(got), reqs, latent),
            [spec((size, width), F32)] + [spec((size, width), BF16)] * (radix - 1),
            [keep] + got,
            name="merge",
        )
        keep = pieces[0]
        got = [swap(pieces[j], count, j * stride) for j in reversed(range(1, radix))]

    parts_out = 4
    model = out_weight.shape[1]
    quarter = model // parts_out
    keep, send = call(
        functools.partial(project_body, 1 + len(got), reqs, heads, latent, parts_out),
        [spec((rows, 2 * quarter), F32), spec((rows, 2 * quarter), BF16)],
        [keep] + got + [value_up, out_weight],
        name="project",
    )
    kept = keep + swap(send, count, stages[0][0]).astype(F32)
    kept = kept[:, :quarter] + swap(kept[:, quarter:].astype(BF16), count, stages[1][0]).astype(F32)
    for stride, radix in stages[2:]:
        mine = kept.astype(BF16)
        terms = [mine.astype(F32)] + [
            swap(mine, count, j * stride).astype(F32) for j in range(1, radix)
        ]
        while len(terms) > 1:
            terms = [terms[i] + terms[i + 1] for i in range(0, len(terms), 2)]
        kept = terms[0]
    done = kept.astype(BF16)
    both = jnp.concatenate([done, swap(done, count, stages[1][0])], axis=1)
    other = swap(both, count, stages[0][0])
    return pl.pallas_call(
        functools.partial(place_body, parts_out),
        out_shape=spec((rows, model), BF16),
        in_specs=[pl.BlockSpec(memory_space=pltpu.VMEM)] * 2,
        out_specs=pl.BlockSpec(memory_space=pl.ANY),
        scratch_shapes=[pltpu.SemaphoreType.DMA((parts_out,))],
        compiler_params=pltpu.CompilerParams(vmem_limit_bytes=16 << 20),
        name="place",
    )(both, other)


def solution(mesh):
    placed = (
        P("groups", None),
        P(),
        P(None, "ctx"),
        P(None, "ctx"),
        P("ctx", None, None),
        P("ctx", None, None),
        P("ctx", None),
        P("groups", "ctx", None),
        P("groups", None, "ctx"),
        P("groups"),
    )
    return jax.shard_map(
        functools.partial(local, mesh.shape["ctx"]),
        mesh=mesh,
        in_specs=placed,
        out_specs=P("groups", None),
        check_vma=False,
    )
```

```python
import functools
import math

import jax
import jax.numpy as jnp
from jax import lax
from jax.experimental import pallas as pl
from jax.experimental.pallas import tpu as pltpu
from jax.sharding import PartitionSpec as P

mscale_yarn = 1.0 + 0.1 * math.log(40.0)
masked_score = -1e30
LOG2E = 1.4426950408889634
LANES = 128
F32 = jnp.float32
BF16 = jnp.bfloat16


def stage_list(count):
    stages, stride = [], 1
    while stride < count:
        left = count // stride
        radix = 2 if (stride < 4 or left < 4) else 4
        stages.append((stride, radix))
        stride *= radix
    return stages


def hop(j, stride):
    return j * stride + (1 if j > 1 else 0)


def beside_rel(e):
    return (e & 1) ^ (3 if e & 2 else 0)


def swap(x, count, mask):
    return lax.ppermute(x, "ctx", [(i, i ^ mask) for i in range(count)])


def call(body, outs, operands, *, flops=0, smem=(), name=None, limit=40 << 20):
    specs = [
        pl.BlockSpec(memory_space=pltpu.SMEM if i in smem else pltpu.VMEM)
        for i in range(len(operands))
    ]
    total = sum(o.size * o.dtype.itemsize for o in list(outs) + list(operands))
    return pl.pallas_call(
        body,
        out_shape=tuple(outs),
        in_specs=specs,
        out_specs=tuple(pl.BlockSpec(memory_space=pltpu.VMEM) for _ in outs),
        compiler_params=pltpu.CompilerParams(vmem_limit_bytes=limit),
        cost_estimate=pl.CostEstimate(flops=flops, bytes_accessed=total, transcendentals=0),
        name=name,
    )(*operands)


def spec(shape, dtype):
    return jax.ShapeDtypeStruct(shape, dtype)


def table_body(keys, table_ref):
    table_ref[...] = (
        lax.axis_index("ctx") * keys
        + lax.broadcasted_iota(jnp.int32, table_ref.shape, 1)
        - lax.broadcasted_iota(jnp.int32, table_ref.shape, 0)
    )


def query_body(heads, reqs, x_ref, gain_ref, nope_ref, rope_ref, key_ref, table_ref, out_ref):
    rows = x_ref.shape[0]
    stretch = rows // reqs
    nope_width, latent = key_ref.shape[1], key_ref.shape[2]
    rope_width = rope_ref.shape[1] // heads
    x = x_ref[...].astype(F32)
    mean = jnp.mean(x * x, axis=-1, keepdims=True)
    normed = (x * lax.rsqrt(mean + 1e-06) * gain_ref[...].astype(F32).reshape(1, -1)).astype(BF16)
    nope = jnp.dot(normed, nope_ref[...], preferred_element_type=F32).astype(BF16)
    rope = jnp.dot(normed, rope_ref[...], preferred_element_type=F32)
    lat = [
        jnp.dot(
            nope[:, h * nope_width : (h + 1) * nope_width], key_ref[h], preferred_element_type=F32
        )
        for h in range(heads)
    ]
    ropes = []
    for b in range(reqs):
        part = slice(b * stretch, (b + 1) * stretch)
        rows_b = jnp.concatenate([lat[h][part] for h in range(heads)], axis=0)
        out_ref[:, b * latent : (b + 1) * latent] = rows_b.astype(BF16)
        ropes.append(
            jnp.concatenate(
                [rope[part, h * rope_width : (h + 1) * rope_width] for h in range(heads)], axis=0
            )
        )
    out_ref[:, reqs * latent :] = jnp.concatenate(ropes, axis=1).astype(BF16)


def pack_stats(columns):
    rows = columns[0].shape[0]
    lane = lax.broadcasted_iota(jnp.int32, (rows, LANES), 1)
    out = jnp.zeros((rows, LANES), F32)
    for b, column in enumerate(columns):
        high = column.astype(BF16).astype(F32)
        rest = column - high
        mid = rest.astype(BF16).astype(F32)
        low = rest - mid
        for k, term in enumerate((high, mid, low)):
            out = jnp.where(lane == 3 * b + k, term, out)
    return out


def read_stats(stats, b):
    return (stats[:, 3 * b : 3 * b + 1] + stats[:, 3 * b + 1 : 3 * b + 2]) + stats[
        :, 3 * b + 2 : 3 * b + 3
    ]


def merge(parts, reqs, latent):
    tops = []
    pooled = []
    for b in range(reqs):
        lse = [read_stats(p[:, reqs * latent :], b) for p in parts]
        top = functools.reduce(jnp.maximum, lse)
        weight = [jnp.exp(m - top) for m in lse]
        total = functools.reduce(jnp.add, weight)
        inverse = 1.0 / total
        value = functools.reduce(
            jnp.add,
            [p[:, b * latent : (b + 1) * latent] * (w * inverse) for p, w in zip(parts, weight)],
        )
        pooled.append(value)
        tops.append(top + jnp.log(total))
    return pooled, tops


def attend_body(
    n_q, reqs, latent, rope_width, stretch, scale, chunk, *refs
):
    length_ref, table_ref, refs = refs[0], refs[1], refs[2:]
    q_refs = refs[:n_q]
    lat_ref, rope_ref = refs[n_q], refs[1 + n_q]
    keep_ref, send_ref = refs[2 + n_q], refs[3 + n_q]
    q_s, s_s, w_s = refs[4 + n_q :]
    rows = q_s.shape[0]
    half = rows // 2
    keys = lat_ref.shape[1]
    at = 0
    for q in q_refs:
        q_s[at : at + q.shape[0], :] = q[...]
        at += q.shape[0]
    block = min(rows, 256)
    for r0 in range(0, rows, block):
        rs = slice(r0, r0 + block)
        stats, peaks = [], []
        for b in range(reqs):
            seen = length_ref[b]
            lhs = q_s[rs, b * latent : (b + 1) * latent]
            base = reqs * latent + b * rope_width
            lhs_rope = q_s[rs, base : base + rope_width]
            peak = None
            for k0 in range(0, keys, chunk):
                s = lax.dot_general(
                    lhs,
                    lat_ref[b, k0 : k0 + chunk, :],
                    (((1,), (1,)), ((), ())),
                    preferred_element_type=F32,
                ) + jnp.dot(
                    lhs_rope, rope_ref[b, :, k0 : k0 + chunk], preferred_element_type=F32
                )
                visible = table_ref[...] + k0 <= seen
                s = jnp.where(
                    visible[None], s.reshape(block // stretch, stretch, chunk), masked_score
                ).reshape(block, chunk)
                s_s[b, :, k0 : k0 + chunk] = s
                top = jnp.max(s, axis=1, keepdims=True)
                peak = top if peak is None else jnp.maximum(peak, top)
            peaks.append(peak)
        for b in range(reqs):
            peak = peaks[b]
            total = None
            for k0 in range(0, keys, chunk):
                w = jnp.exp2((s_s[b, :, k0 : k0 + chunk] - peak) * (scale * LOG2E))
                part = jnp.sum(w, axis=1, keepdims=True)
                total = part if total is None else total + part
                w_s[b, :, k0 : k0 + chunk] = w.astype(BF16)
            pool = jnp.dot(w_s[b], lat_ref[b], preferred_element_type=F32)
            pool = pool * (1.0 / total)
            stats.append(peak * scale + jnp.log(total))
            cols = slice(b * latent, (b + 1) * latent)
            for lo in range(r0, r0 + block, min(block, half)):
                size = min(block, half)
                piece = pool[lo - r0 : lo - r0 + size]
                if lo < half:
                    keep_ref[lo : lo + size, cols] = piece
                else:
                    send_ref[lo - half : lo - half + size, cols] = piece.astype(BF16)
        packed = pack_stats(stats)
        for lo in range(r0, r0 + block, min(block, half)):
            size = min(block, half)
            piece = packed[lo - r0 : lo - r0 + size]
            if lo < half:
                keep_ref[lo : lo + size, reqs * latent :] = piece
            else:
                send_ref[lo - half : lo - half + size, reqs * latent :] = piece.astype(BF16)


def merge_body(n_in, reqs, latent, *refs):
    parts = [r[...].astype(F32) for r in refs[:n_in]]
    outs = refs[n_in:]
    pooled, tops = merge(parts, reqs, latent)
    packed = pack_stats(tops)
    size = outs[0].shape[0]
    for j, out in enumerate(outs):
        rows = slice(j * size, (j + 1) * size)
        for b in range(reqs):
            out[:, b * latent : (b + 1) * latent] = pooled[b][rows].astype(out.dtype)
        out[:, reqs * latent :] = packed[rows].astype(out.dtype)


def project_body(n_in, reqs, heads, latent, parts_out, *refs):
    parts = [r[...].astype(F32) for r in refs[:n_in]]
    value_ref, weight_ref = refs[n_in], refs[n_in + 1]
    keep_ref, send_ref = refs[n_in + 2], refs[n_in + 3]
    pooled, _ = merge(parts, reqs, latent)
    stretch = pooled[0].shape[0] // heads
    values = []
    for h in range(heads):
        rows = jnp.concatenate([p[h * stretch : (h + 1) * stretch] for p in pooled], axis=0)
        values.append(
            jnp.dot(rows.astype(BF16), value_ref[h], preferred_element_type=F32).astype(BF16)
        )
    hidden = jnp.concatenate(values, axis=1)
    mine = lax.rem(lax.axis_index("ctx"), parts_out)
    width = weight_ref.shape[1] // parts_out
    for e in range(parts_out):
        start = pl.multiple_of(jnp.bitwise_xor(mine, beside_rel(e)) * width, LANES)
        out = jnp.dot(hidden, weight_ref[:, pl.ds(start, width)], preferred_element_type=F32)
        slot = slice((e // 2) * width, (e // 2 + 1) * width)
        if e % 2 == 0:
            keep_ref[:, slot] = out
        else:
            send_ref[:, slot] = out.astype(BF16)


def join_body(*refs):
    at = 0
    for r in refs[:-1]:
        refs[-1][at : at + r.shape[0], :] = r[...]
        at += r.shape[0]


def place_body(parts_out, *refs):
    pieces, out_ref, sems = refs[:-2], refs[-2], refs[-1]
    copies = []
    mine = lax.rem(lax.axis_index("ctx"), parts_out)
    width = out_ref.shape[1] // parts_out
    e_order = (0, 2, 1, 3)
    at = 0
    for piece in pieces:
        for k in range(piece.shape[1] // width):
            start = pl.multiple_of(jnp.bitwise_xor(mine, beside_rel(e_order[at])) * width, LANES)
            copies.append(
                pltpu.make_async_copy(
                    piece.at[:, pl.ds(k * width, width)],
                    out_ref.at[:, pl.ds(start, width)],
                    sems.at[at],
                )
            )
            copies[-1].start()
            at += 1
    for copy in copies:
        copy.wait()


def local(count, query_input, query_gain, nope_weight, rope_weight, key_up, value_up, out_weight,
          cache_latent, cache_rope, cached_length):
    heads, nope_width, latent = key_up.shape
    reqs = cache_latent.shape[0]
    rope_width = cache_rope.shape[1]
    rows = query_input.shape[0]
    stretch = rows // reqs
    own = heads * stretch
    width = reqs * latent + LANES
    stages = stage_list(count)
    scale = mscale_yarn * mscale_yarn / math.sqrt(nope_width + rope_width)

    chunk = 256
    (table,) = call(
        functools.partial(table_body, cache_latent.shape[1]),
        [spec((stretch, chunk), jnp.int32)],
        [],
        flops=2 << 30,
        limit=16 << 20,
        name="table",
    )
    (query,) = call(
        functools.partial(query_body, heads, reqs),
        [spec((own, width), BF16)],
        [query_input, query_gain, nope_weight, rope_weight, key_up, table],
        limit=16 << 20,
        name="query",
    )
    join_flops = 4 << 30
    held = query
    for stride, radix in reversed(stages[2:]):
        got = [swap(held, count, hop(j, stride)) for j in range(1, radix)]
        parts = [held] + got
        (held,) = call(
            join_body,
            [spec((radix * held.shape[0], width), BF16)],
            parts,
            flops=join_flops,
            limit=16 << 20,
            name="join",
        )
    beside = swap(held, count, stages[1][0])
    near = jnp.concatenate([held, beside], axis=0)
    far = swap(near, count, stages[0][0])

    half = near.shape[0]
    total = 2 * half
    block = min(total, 256)
    operands = [cached_length, table, near, far, cache_latent, cache_rope]
    keep, send = pl.pallas_call(
        functools.partial(attend_body, 2, reqs, latent, rope_width, stretch, scale, chunk),
        out_shape=(spec((half, width), F32), spec((half, width), BF16)),
        in_specs=[pl.BlockSpec(memory_space=pltpu.SMEM)]
        + [pl.BlockSpec(memory_space=pltpu.VMEM)] * 5,
        out_specs=(pl.BlockSpec(memory_space=pltpu.VMEM),) * 2,
        scratch_shapes=[
            pltpu.VMEM((total, width), BF16),
            pltpu.VMEM((reqs, block, cache_latent.shape[1]), F32),
            pltpu.VMEM((reqs, block, cache_latent.shape[1]), BF16),
        ],
        compiler_params=pltpu.CompilerParams(vmem_limit_bytes=48 << 20),
        cost_estimate=pl.CostEstimate(
            flops=4 * total * cache_latent.shape[1] * latent * reqs,
            bytes_accessed=8 << 20,
            transcendentals=0,
        ),
        name="attend",
    )(*operands)

    got = [swap(send, count, stages[0][0])]
    for stride, radix in stages[1:]:
        size = keep.shape[0] // radix
        pieces = call(
            functools.partial(merge_body, 1 + len(got), reqs, latent),
            [spec((size, width), F32)] + [spec((size, width), BF16)] * (radix - 1),
            [keep] + got,
            name="merge",
        )
        keep = pieces[0]
        got = [swap(pieces[j], count, hop(j, stride)) for j in reversed(range(1, radix))]

    parts_out = 4
    model = out_weight.shape[1]
    quarter = model // parts_out
    keep, send = call(
        functools.partial(project_body, 1 + len(got), reqs, heads, latent, parts_out),
        [spec((rows, 2 * quarter), F32), spec((rows, 2 * quarter), BF16)],
        [keep] + got + [value_up, out_weight],
        name="project",
    )
    kept = keep + swap(send, count, stages[0][0]).astype(F32)
    kept = kept[:, :quarter] + swap(kept[:, quarter:].astype(BF16), count, beside_rel(2)).astype(F32)
    for stride, radix in stages[2:]:
        mine = kept.astype(BF16)
        terms = [mine.astype(F32)] + [
            swap(mine, count, j * stride).astype(F32) for j in range(1, radix)
        ]
        while len(terms) > 1:
            terms = [terms[i] + terms[i + 1] for i in range(0, len(terms), 2)]
        kept = terms[0]
    done = kept.astype(BF16)
    both = jnp.concatenate([done, swap(done, count, beside_rel(2))], axis=1)
    other = swap(both, count, stages[0][0])
    return pl.pallas_call(
        functools.partial(place_body, parts_out),
        out_shape=spec((rows, model), BF16),
        in_specs=[pl.BlockSpec(memory_space=pltpu.VMEM)] * 2,
        out_specs=pl.BlockSpec(memory_space=pl.ANY),
        scratch_shapes=[pltpu.SemaphoreType.DMA((parts_out,))],
        compiler_params=pltpu.CompilerParams(vmem_limit_bytes=16 << 20),
        name="place",
    )(both, other)


def solution(mesh):
    placed = (
        P("groups", None),
        P(),
        P(None, "ctx"),
        P(None, "ctx"),
        P("ctx", None, None),
        P("ctx", None, None),
        P("ctx", None),
        P("groups", "ctx", None),
        P("groups", None, "ctx"),
        P("groups"),
    )
    return jax.shard_map(
        functools.partial(local, mesh.shape["ctx"]),
        mesh=mesh,
        in_specs=placed,
        out_specs=P("groups", None),
        check_vma=False,
    )
```

```python
import functools
import math

import jax
import jax.numpy as jnp
from jax import lax
from jax.experimental import pallas as pl
from jax.experimental.pallas import tpu as pltpu
from jax.sharding import PartitionSpec as P

mscale_yarn = 1.0 + 0.1 * math.log(40.0)
masked_score = -1e30
LOG2E = 1.4426950408889634
LANES = 128
F32 = jnp.float32
BF16 = jnp.bfloat16


def stage_list(count):
    stages, stride = [], 1
    while stride < count:
        left = count // stride
        radix = 2 if (stride < 4 or left < 4) else 4
        stages.append((stride, radix))
        stride *= radix
    return stages


def swap(x, count, mask):
    return lax.ppermute(x, "ctx", [(i, i ^ mask) for i in range(count)])


def call(body, outs, operands, *, flops=0, smem=(), name=None, limit=40 << 20):
    specs = [
        pl.BlockSpec(memory_space=pltpu.SMEM if i in smem else pltpu.VMEM)
        for i in range(len(operands))
    ]
    total = sum(o.size * o.dtype.itemsize for o in list(outs) + list(operands))
    return pl.pallas_call(
        body,
        out_shape=tuple(outs),
        in_specs=specs,
        out_specs=tuple(pl.BlockSpec(memory_space=pltpu.VMEM) for _ in outs),
        compiler_params=pltpu.CompilerParams(vmem_limit_bytes=limit),
        cost_estimate=pl.CostEstimate(flops=flops, bytes_accessed=total, transcendentals=0),
        name=name,
    )(*operands)


def spec(shape, dtype):
    return jax.ShapeDtypeStruct(shape, dtype)


def table_body(keys, table_ref):
    table_ref[...] = (
        lax.axis_index("ctx") * keys
        + lax.broadcasted_iota(jnp.int32, table_ref.shape, 1)
        - lax.broadcasted_iota(jnp.int32, table_ref.shape, 0)
    )


def query_body(heads, reqs, x_ref, gain_ref, nope_ref, rope_ref, key_ref, table_ref, out_ref):
    rows = x_ref.shape[0]
    stretch = rows // reqs
    nope_width, latent = key_ref.shape[1], key_ref.shape[2]
    rope_width = rope_ref.shape[1] // heads
    x = x_ref[...].astype(F32)
    mean = jnp.mean(x * x, axis=-1, keepdims=True)
    normed = (x * lax.rsqrt(mean + 1e-06) * gain_ref[...].astype(F32).reshape(1, -1)).astype(BF16)
    nope = jnp.dot(normed, nope_ref[...], preferred_element_type=F32).astype(BF16)
    rope = jnp.dot(normed, rope_ref[...], preferred_element_type=F32)
    lat = [
        jnp.dot(
            nope[:, h * nope_width : (h + 1) * nope_width], key_ref[h], preferred_element_type=F32
        )
        for h in range(heads)
    ]
    for b in range(reqs):
        part = slice(b * stretch, (b + 1) * stretch)
        rows_b = jnp.concatenate([lat[h][part] for h in range(heads)], axis=0)
        at = b * (latent + LANES)
        out_ref[:, at : at + latent] = rows_b.astype(BF16)
        rows_b = jnp.concatenate(
            [rope[part, h * rope_width : (h + 1) * rope_width] for h in range(heads)],
            axis=0,
        )
        rows_b = jnp.concatenate(
            [rows_b, jnp.zeros((heads * stretch, LANES - rope_width), F32)], axis=1
        )
        out_ref[:, at + latent : at + latent + LANES] = rows_b.astype(BF16)


def pack_stats(column):
    rows = column.shape[0]
    lane = lax.broadcasted_iota(jnp.int32, (rows, LANES), 1)
    high = column.astype(BF16).astype(F32)
    rest = column - high
    mid = rest.astype(BF16).astype(F32)
    out = jnp.zeros((rows, LANES), F32)
    for k, term in enumerate((high, mid, rest - mid)):
        out = jnp.where(lane == k, term, out)
    return out


def merge(parts):
    latent = parts[0].shape[1] - LANES
    lse = [
        (p[:, latent : latent + 1] + p[:, latent + 1 : latent + 2]) + p[:, latent + 2 : latent + 3]
        for p in parts
    ]
    top = functools.reduce(jnp.maximum, lse)
    weight = [jnp.exp(m - top) for m in lse]
    total = functools.reduce(jnp.add, weight)
    inverse = 1.0 / total
    pooled = functools.reduce(
        jnp.add, [p[:, :latent] * (w * inverse) for p, w in zip(parts, weight)]
    )
    return pooled, top + jnp.log(total)


def attend_body(b, latent, rope_width, stretch, scale, chunk, *refs):
    length_ref, table_ref, near_ref, far_ref = refs[:4]
    lat_ref, key_ref, keep_ref, send_ref, q_s, r_s, s_s, w_s = refs[4:]
    half = near_ref.shape[0]
    rows = 2 * half
    keys = lat_ref.shape[1]
    for at, q in ((0, near_ref), (half, far_ref)):
        q_s[at : at + half, :] = q[:, :latent]
        r_s[at : at + half, :] = q[:, latent : latent + rope_width]
    block = min(rows, 256)
    step = min(block, half)
    seen = length_ref[b]
    for r0 in range(0, rows, block):
        lhs = q_s[r0 : r0 + block, :]
        lhs_rope = r_s[r0 : r0 + block, :]
        peak = None
        for k0 in range(0, keys, chunk):
            s = lax.dot_general(
                lhs,
                lat_ref[b, k0 : k0 + chunk, :],
                (((1,), (1,)), ((), ())),
                preferred_element_type=F32,
            ) + jnp.dot(lhs_rope, key_ref[b, :, k0 : k0 + chunk], preferred_element_type=F32)
            visible = table_ref[...] + k0 <= seen
            s = jnp.where(
                visible[None], s.reshape(block // stretch, stretch, chunk), masked_score
            ).reshape(block, chunk)
            s_s[:, k0 : k0 + chunk] = s
            top = jnp.max(s, axis=1, keepdims=True)
            peak = top if peak is None else jnp.maximum(peak, top)
        total = None
        for k0 in range(0, keys, chunk):
            w = jnp.exp2((s_s[:, k0 : k0 + chunk] - peak) * (scale * LOG2E))
            part = jnp.sum(w, axis=1, keepdims=True)
            total = part if total is None else total + part
            w_s[:, k0 : k0 + chunk] = w.astype(BF16)
        pool = jnp.dot(w_s[...], lat_ref[b], preferred_element_type=F32) * (1.0 / total)
        packed = pack_stats(peak * scale + jnp.log(total))
        for lo in range(r0, r0 + block, step):
            part = slice(lo - r0, lo - r0 + step)
            if lo < half:
                keep_ref[lo : lo + step, :latent] = pool[part]
                keep_ref[lo : lo + step, latent:] = packed[part]
            else:
                send_ref[lo - half : lo - half + step, :latent] = pool[part].astype(BF16)
                send_ref[lo - half : lo - half + step, latent:] = packed[part].astype(BF16)


def read_groups(groups, width, refs):
    return [
        [refs[i][:, slot * width : (slot + 1) * width].astype(F32) for i, slot in group]
        for group in groups
    ]


def merge_body(n_in, groups, width, *refs):
    outs = refs[n_in:]
    size = outs[0].shape[0]
    for g, parts in enumerate(read_groups(groups, width, refs)):
        pooled, top = merge(parts)
        packed = pack_stats(top)
        at = g * width
        for j, out in enumerate(outs):
            rows = slice(j * size, (j + 1) * size)
            out[:, at : at + width - LANES] = pooled[rows].astype(out.dtype)
            out[:, at + width - LANES : at + width] = packed[rows].astype(out.dtype)


def project_body(n_in, groups, width, heads, parts_out, *refs):
    value_ref, weight_ref = refs[n_in], refs[n_in + 1]
    keep_ref, send_ref = refs[n_in + 2], refs[n_in + 3]
    pooled = [merge(parts)[0] for parts in read_groups(groups, width, refs)]
    stretch = pooled[0].shape[0] // heads
    values = []
    for h in range(heads):
        rows = jnp.concatenate([p[h * stretch : (h + 1) * stretch] for p in pooled], axis=0)
        values.append(
            jnp.dot(rows.astype(BF16), value_ref[h], preferred_element_type=F32).astype(BF16)
        )
    hidden = jnp.concatenate(values, axis=1)
    mine = lax.rem(lax.axis_index("ctx"), parts_out)
    columns = weight_ref.shape[1] // parts_out
    for e in range(parts_out):
        start = pl.multiple_of(jnp.bitwise_xor(mine, e) * columns, LANES)
        out = jnp.dot(hidden, weight_ref[:, pl.ds(start, columns)], preferred_element_type=F32)
        slot = slice((e // 2) * columns, (e // 2 + 1) * columns)
        if e % 2 == 0:
            keep_ref[:, slot] = out
        else:
            send_ref[:, slot] = out.astype(BF16)


def join_body(n_in, lanes, *refs):
    at = 0
    for r in refs[:n_in]:
        for out, cols in zip(refs[n_in:], lanes):
            out[at : at + r.shape[0], :] = r[:, cols]
        at += r.shape[0]


def place_body(parts_out, *refs):
    pieces, out_ref, sems = refs[:-2], refs[-2], refs[-1]
    copies = []
    mine = lax.rem(lax.axis_index("ctx"), parts_out)
    width = out_ref.shape[1] // parts_out
    e_order = (0, 2, 1, 3)
    at = 0
    for piece in pieces:
        for k in range(piece.shape[1] // width):
            start = pl.multiple_of(jnp.bitwise_xor(mine, e_order[at]) * width, LANES)
            copies.append(
                pltpu.make_async_copy(
                    piece.at[:, pl.ds(k * width, width)],
                    out_ref.at[:, pl.ds(start, width)],
                    sems.at[at],
                )
            )
            copies[-1].start()
            at += 1
    for copy in copies:
        copy.wait()


def local(count, query_input, query_gain, nope_weight, rope_weight, key_up, value_up, out_weight,
          cache_latent, cache_rope, cached_length):
    heads, nope_width, latent = key_up.shape
    reqs = cache_latent.shape[0]
    rope_width = cache_rope.shape[1]
    rows = query_input.shape[0]
    stretch = rows // reqs
    own = heads * stretch
    each = latent + LANES
    width = reqs * each
    stages = stage_list(count)
    scale = mscale_yarn * mscale_yarn / math.sqrt(nope_width + rope_width)

    chunk = 256
    (table,) = call(
        functools.partial(table_body, cache_latent.shape[1]),
        [spec((stretch, chunk), jnp.int32)],
        [],
        flops=2 << 30,
        limit=16 << 20,
        name="table",
    )
    (query,) = call(
        functools.partial(query_body, heads, reqs),
        [spec((own, width), BF16)],
        [query_input, query_gain, nope_weight, rope_weight, key_up, table],
        limit=16 << 20,
        name="query",
    )
    spans = [slice(b * each, (b + 1) * each) for b in range(reqs)]
    gathered = [query]
    for at, (stride, radix) in enumerate(reversed(stages[2:])):
        (held,) = gathered
        got = [swap(held, count, j * stride) for j in range(1, radix)]
        lanes = spans if at == len(stages) - 3 else [slice(0, width)]
        gathered = call(
            functools.partial(join_body, radix, lanes),
            [spec((radix * held.shape[0], c.stop - c.start), BF16) for c in lanes],
            [held] + got,
            flops=4 << 30,
            limit=16 << 20,
            name="join",
        )
    near, far = [], []
    for held in gathered:
        near.append(jnp.concatenate([held, swap(held, count, stages[1][0])], axis=0))
        far.append(swap(near[-1], count, stages[0][0]))

    half = near[0].shape[0]
    total = 2 * half
    block = min(total, 256)
    keys = cache_latent.shape[1]
    keeps, gots = [], []
    for b in range(reqs):
        operands = [cached_length, table, near[b], far[b], cache_latent, cache_rope]
        keep, send = pl.pallas_call(
            functools.partial(attend_body, b, latent, rope_width, stretch, scale, chunk),
            out_shape=(spec((half, each), F32), spec((half, each), BF16)),
            in_specs=[pl.BlockSpec(memory_space=pltpu.SMEM)]
            + [pl.BlockSpec(memory_space=pltpu.VMEM)] * (len(operands) - 1),
            out_specs=(pl.BlockSpec(memory_space=pltpu.VMEM),) * 2,
            scratch_shapes=[
                pltpu.VMEM((total, latent), BF16),
                pltpu.VMEM((total, rope_width), BF16),
                pltpu.VMEM((block, keys), F32),
                pltpu.VMEM((block, keys), BF16),
            ],
            compiler_params=pltpu.CompilerParams(vmem_limit_bytes=32 << 20),
            cost_estimate=pl.CostEstimate(
                flops=4 * total * keys * latent, bytes_accessed=4 << 20, transcendentals=0
            ),
            name="attend",
        )(*operands)
        keeps.append(keep)
        gots.append(swap(send, count, stages[0][0]))

    stride, radix = stages[1]
    size = half // radix
    for b in range(reqs):
        keeps[b], send = call(
            functools.partial(merge_body, 2, [[(0, 0), (1, 0)]], each),
            [spec((size, each), F32), spec((size, each), BF16)],
            [keeps[b], gots[b]],
            limit=16 << 20,
            name="merge",
        )
        gots[b] = swap(send, count, stride)
    operands = [x for b in range(reqs) for x in (keeps[b], gots[b])]
    groups = [[(2 * b, 0), (2 * b + 1, 0)] for b in range(reqs)]
    for stride, radix in stages[2:]:
        size //= radix
        pieces = call(
            functools.partial(merge_body, len(operands), groups, each),
            [spec((size, reqs * each), F32)] + [spec((size, reqs * each), BF16)] * (radix - 1),
            operands,
            limit=16 << 20,
            name="merge",
        )
        got = [swap(pieces[j], count, j * stride) for j in reversed(range(1, radix))]
        operands = [pieces[0]] + got
        groups = [[(i, b) for i in range(radix)] for b in range(reqs)]

    parts_out = 4
    model = out_weight.shape[1]
    quarter = model // parts_out
    keep, send = call(
        functools.partial(project_body, len(operands), groups, each, heads, parts_out),
        [spec((rows, 2 * quarter), F32), spec((rows, 2 * quarter), BF16)],
        operands + [value_up, out_weight],
        name="project",
    )
    kept = keep + swap(send, count, stages[0][0]).astype(F32)
    kept = kept[:, :quarter] + swap(kept[:, quarter:].astype(BF16), count, stages[1][0]).astype(F32)
    for stride, radix in stages[2:]:
        mine = kept.astype(BF16)
        terms = [mine.astype(F32)] + [
            swap(mine, count, j * stride).astype(F32) for j in range(1, radix)
        ]
        while len(terms) > 1:
            terms = [terms[i] + terms[i + 1] for i in range(0, len(terms), 2)]
        kept = terms[0]
    done = kept.astype(BF16)
    both = jnp.concatenate([done, swap(done, count, stages[1][0])], axis=1)
    other = swap(both, count, stages[0][0])
    return pl.pallas_call(
        functools.partial(place_body, parts_out),
        out_shape=spec((rows, model), BF16),
        in_specs=[pl.BlockSpec(memory_space=pltpu.VMEM)] * 2,
        out_specs=pl.BlockSpec(memory_space=pl.ANY),
        scratch_shapes=[pltpu.SemaphoreType.DMA((parts_out,))],
        compiler_params=pltpu.CompilerParams(vmem_limit_bytes=16 << 20),
        name="place",
    )(both, other)


def solution(mesh):
    placed = (
        P("groups", None),
        P(),
        P(None, "ctx"),
        P(None, "ctx"),
        P("ctx", None, None),
        P("ctx", None, None),
        P("ctx", None),
        P("groups", "ctx", None),
        P("groups", None, "ctx"),
        P("groups"),
    )
    return jax.shard_map(
        functools.partial(local, mesh.shape["ctx"]),
        mesh=mesh,
        in_specs=placed,
        out_specs=P("groups", None),
        check_vma=False,
    )
```

```python
import functools
import math

import jax
import jax.numpy as jnp
from jax import lax
from jax.experimental import pallas as pl
from jax.experimental.pallas import tpu as pltpu
from jax.sharding import PartitionSpec as P

mscale_yarn = 1.0 + 0.1 * math.log(40.0)
masked_score = -1e30
LOG2E = 1.4426950408889634
LANES = 128
F32 = jnp.float32
BF16 = jnp.bfloat16


def stage_list(count):
    stages, stride = [], 1
    while stride < count:
        left = count // stride
        radix = 2 if (stride < 4 or left < 4) else 4
        stages.append((stride, radix))
        stride *= radix
    return stages


def swap(x, count, mask):
    return lax.ppermute(x, "ctx", [(i, i ^ mask) for i in range(count)])


def call(body, outs, operands, *, flops=0, smem=(), name=None, limit=40 << 20):
    specs = [
        pl.BlockSpec(memory_space=pltpu.SMEM if i in smem else pltpu.VMEM)
        for i in range(len(operands))
    ]
    total = sum(o.size * o.dtype.itemsize for o in list(outs) + list(operands))
    return pl.pallas_call(
        body,
        out_shape=tuple(outs),
        in_specs=specs,
        out_specs=tuple(pl.BlockSpec(memory_space=pltpu.VMEM) for _ in outs),
        compiler_params=pltpu.CompilerParams(vmem_limit_bytes=limit),
        cost_estimate=pl.CostEstimate(flops=flops, bytes_accessed=total, transcendentals=0),
        name=name,
    )(*operands)


def spec(shape, dtype):
    return jax.ShapeDtypeStruct(shape, dtype)


def table_body(keys, table_ref):
    table_ref[...] = (
        lax.axis_index("ctx") * keys
        + lax.broadcasted_iota(jnp.int32, table_ref.shape, 1)
        - lax.broadcasted_iota(jnp.int32, table_ref.shape, 0)
    )


def query_body(heads, reqs, x_ref, gain_ref, nope_ref, rope_ref, key_ref, table_ref, out_ref):
    rows = x_ref.shape[0]
    stretch = rows // reqs
    nope_width, latent = key_ref.shape[1], key_ref.shape[2]
    rope_width = rope_ref.shape[1] // heads
    x = x_ref[...].astype(F32)
    mean = jnp.mean(x * x, axis=-1, keepdims=True)
    normed = (x * lax.rsqrt(mean + 1e-06) * gain_ref[...].astype(F32).reshape(1, -1)).astype(BF16)
    nope = jnp.dot(normed, nope_ref[...], preferred_element_type=F32).astype(BF16)
    rope = jnp.dot(normed, rope_ref[...], preferred_element_type=F32)
    lat = [
        jnp.dot(
            nope[:, h * nope_width : (h + 1) * nope_width], key_ref[h], preferred_element_type=F32
        )
        for h in range(heads)
    ]
    ropes = []
    for b in range(reqs):
        part = slice(b * stretch, (b + 1) * stretch)
        rows_b = jnp.concatenate([lat[h][part] for h in range(heads)], axis=0)
        out_ref[:, b * latent : (b + 1) * latent] = rows_b.astype(BF16)
        ropes.append(
            jnp.concatenate(
                [rope[part, h * rope_width : (h + 1) * rope_width] for h in range(heads)], axis=0
            )
        )
    out_ref[:, reqs * latent :] = jnp.concatenate(ropes, axis=1).astype(BF16)


def pack_stats(columns):
    rows = columns[0].shape[0]
    lane = lax.broadcasted_iota(jnp.int32, (rows, LANES), 1)
    out = jnp.zeros((rows, LANES), F32)
    for b, column in enumerate(columns):
        high = column.astype(BF16).astype(F32)
        rest = column - high
        mid = rest.astype(BF16).astype(F32)
        low = rest - mid
        for k, term in enumerate((high, mid, low)):
            out = jnp.where(lane == 3 * b + k, term, out)
    return out


def read_stats(stats, b):
    return (stats[:, 3 * b : 3 * b + 1] + stats[:, 3 * b + 1 : 3 * b + 2]) + stats[
        :, 3 * b + 2 : 3 * b + 3
    ]


def merge(parts, reqs, latent):
    tops = []
    pooled = []
    for b in range(reqs):
        lse = [read_stats(p[:, reqs * latent :], b) for p in parts]
        top = functools.reduce(jnp.maximum, lse)
        weight = [jnp.exp(m - top) for m in lse]
        total = functools.reduce(jnp.add, weight)
        inverse = 1.0 / total
        value = functools.reduce(
            jnp.add,
            [p[:, b * latent : (b + 1) * latent] * (w * inverse) for p, w in zip(parts, weight)],
        )
        pooled.append(value)
        tops.append(top + jnp.log(total))
    return pooled, tops


def attend_body(
    n_q, reqs, latent, rope_width, stretch, scale, chunk, *refs
):
    length_ref, table_ref, refs = refs[0], refs[1], refs[2:]
    q_refs = refs[:n_q]
    lat_ref, rope_ref = refs[n_q], refs[1 + n_q]
    keep_ref, send_ref = refs[2 + n_q], refs[3 + n_q]
    q_s, s_s, w_s = refs[4 + n_q :]
    rows = q_s.shape[0]
    half = rows // 2
    keys = lat_ref.shape[1]
    at = 0
    for q in q_refs:
        q_s[at : at + q.shape[0], :] = q[...]
        at += q.shape[0]
    block = min(rows, 256)
    for r0 in range(0, rows, block):
        rs = slice(r0, r0 + block)
        stats, peaks = [], []
        for b in range(reqs):
            seen = length_ref[b]
            lhs = q_s[rs, b * latent : (b + 1) * latent]
            base = reqs * latent + b * rope_width
            lhs_rope = q_s[rs, base : base + rope_width]
            peak = None
            for k0 in range(0, keys, chunk):
                s = lax.dot_general(
                    lhs,
                    lat_ref[b, k0 : k0 + chunk, :],
                    (((1,), (1,)), ((), ())),
                    preferred_element_type=F32,
                ) + jnp.dot(
                    lhs_rope, rope_ref[b, :, k0 : k0 + chunk], preferred_element_type=F32
                )
                visible = table_ref[...] + k0 <= seen
                s = jnp.where(
                    visible[None], s.reshape(block // stretch, stretch, chunk), masked_score
                ).reshape(block, chunk)
                s_s[b, :, k0 : k0 + chunk] = s
                top = jnp.max(s, axis=1, keepdims=True)
                peak = top if peak is None else jnp.maximum(peak, top)
            peaks.append(peak)
        for b in range(reqs):
            peak = peaks[b]
            total = None
            for k0 in range(0, keys, chunk):
                w = jnp.exp2((s_s[b, :, k0 : k0 + chunk] - peak) * (scale * LOG2E))
                part = jnp.sum(w, axis=1, keepdims=True)
                total = part if total is None else total + part
                w_s[b, :, k0 : k0 + chunk] = w.astype(BF16)
            pool = jnp.dot(w_s[b], lat_ref[b], preferred_element_type=F32)
            pool = pool * (1.0 / total)
            stats.append(peak * scale + jnp.log(total))
            cols = slice(b * latent, (b + 1) * latent)
            for lo in range(r0, r0 + block, min(block, half)):
                size = min(block, half)
                piece = pool[lo - r0 : lo - r0 + size]
                if lo < half:
                    keep_ref[lo : lo + size, cols] = piece
                else:
                    send_ref[lo - half : lo - half + size, cols] = piece.astype(BF16)
        packed = pack_stats(stats)
        for lo in range(r0, r0 + block, min(block, half)):
            size = min(block, half)
            piece = packed[lo - r0 : lo - r0 + size]
            if lo < half:
                keep_ref[lo : lo + size, reqs * latent :] = piece
            else:
                send_ref[lo - half : lo - half + size, reqs * latent :] = piece.astype(BF16)


def merge_body(n_in, reqs, latent, *refs):
    outs = refs[n_in:]
    size = outs[0].shape[0]
    for j, out in enumerate(outs, 1):
        rows = slice(j * size, (j + 1) * size)
        pooled, tops = merge([r[rows, :].astype(F32) for r in refs[:n_in]], reqs, latent)
        for b in range(reqs):
            out[:, b * latent : (b + 1) * latent] = pooled[b].astype(out.dtype)
        out[:, reqs * latent :] = pack_stats(tops).astype(out.dtype)


def project_body(n_in, reqs, heads, latent, parts_out, *refs):
    own = heads * (refs[-1].shape[0] // reqs)
    parts = [r[:own, :].astype(F32) for r in refs[:n_in]]
    value_ref, weight_ref = refs[n_in], refs[n_in + 1]
    keep_ref, send_ref = refs[n_in + 2], refs[n_in + 3]
    pooled, _ = merge(parts, reqs, latent)
    stretch = pooled[0].shape[0] // heads
    values = []
    for h in range(heads):
        rows = jnp.concatenate([p[h * stretch : (h + 1) * stretch] for p in pooled], axis=0)
        values.append(
            jnp.dot(rows.astype(BF16), value_ref[h], preferred_element_type=F32).astype(BF16)
        )
    hidden = jnp.concatenate(values, axis=1)
    mine = lax.rem(lax.axis_index("ctx"), parts_out)
    width = weight_ref.shape[1] // parts_out
    for e in range(parts_out):
        start = pl.multiple_of(jnp.bitwise_xor(mine, e) * width, LANES)
        out = jnp.dot(hidden, weight_ref[:, pl.ds(start, width)], preferred_element_type=F32)
        slot = slice((e // 2) * width, (e // 2 + 1) * width)
        if e % 2 == 0:
            keep_ref[:, slot] = out
        else:
            send_ref[:, slot] = out.astype(BF16)


def join_body(*refs):
    at = 0
    for r in refs[:-1]:
        refs[-1][at : at + r.shape[0], :] = r[...]
        at += r.shape[0]


def place_body(parts_out, *refs):
    pieces, out_ref, sems = refs[:-2], refs[-2], refs[-1]
    copies = []
    mine = lax.rem(lax.axis_index("ctx"), parts_out)
    width = out_ref.shape[1] // parts_out
    e_order = (0, 2, 1, 3)
    at = 0
    for piece in pieces:
        for k in range(piece.shape[1] // width):
            start = pl.multiple_of(jnp.bitwise_xor(mine, e_order[at]) * width, LANES)
            copies.append(
                pltpu.make_async_copy(
                    piece.at[:, pl.ds(k * width, width)],
                    out_ref.at[:, pl.ds(start, width)],
                    sems.at[at],
                )
            )
            copies[-1].start()
            at += 1
    for copy in copies:
        copy.wait()


def local(count, query_input, query_gain, nope_weight, rope_weight, key_up, value_up, out_weight,
          cache_latent, cache_rope, cached_length):
    heads, nope_width, latent = key_up.shape
    reqs = cache_latent.shape[0]
    rope_width = cache_rope.shape[1]
    rows = query_input.shape[0]
    stretch = rows // reqs
    own = heads * stretch
    width = reqs * latent + LANES
    stages = stage_list(count)
    scale = mscale_yarn * mscale_yarn / math.sqrt(nope_width + rope_width)

    chunk = 256
    (table,) = call(
        functools.partial(table_body, cache_latent.shape[1]),
        [spec((stretch, chunk), jnp.int32)],
        [],
        flops=2 << 30,
        limit=16 << 20,
        name="table",
    )
    (query,) = call(
        functools.partial(query_body, heads, reqs),
        [spec((own, width), BF16)],
        [query_input, query_gain, nope_weight, rope_weight, key_up, table],
        limit=16 << 20,
        name="query",
    )
    join_flops = 4 << 30
    held = query
    for stride, radix in reversed(stages[2:]):
        got = [swap(held, count, j * stride) for j in range(1, radix)]
        parts = [held] + got
        (held,) = call(
            join_body,
            [spec((radix * held.shape[0], width), BF16)],
            parts,
            flops=join_flops,
            limit=16 << 20,
            name="join",
        )
    beside = swap(held, count, stages[1][0])
    near = jnp.concatenate([held, beside], axis=0)
    far = swap(near, count, stages[0][0])

    half = near.shape[0]
    total = 2 * half
    block = min(total, 256)
    operands = [cached_length, table, near, far, cache_latent, cache_rope]
    keep, send = pl.pallas_call(
        functools.partial(attend_body, 2, reqs, latent, rope_width, stretch, scale, chunk),
        out_shape=(spec((half, width), F32), spec((half, width), BF16)),
        in_specs=[pl.BlockSpec(memory_space=pltpu.SMEM)]
        + [pl.BlockSpec(memory_space=pltpu.VMEM)] * 5,
        out_specs=(pl.BlockSpec(memory_space=pltpu.VMEM),) * 2,
        scratch_shapes=[
            pltpu.VMEM((total, width), BF16),
            pltpu.VMEM((reqs, block, cache_latent.shape[1]), F32),
            pltpu.VMEM((reqs, block, cache_latent.shape[1]), BF16),
        ],
        compiler_params=pltpu.CompilerParams(vmem_limit_bytes=48 << 20),
        cost_estimate=pl.CostEstimate(
            flops=4 * total * cache_latent.shape[1] * latent * reqs,
            bytes_accessed=8 << 20,
            transcendentals=0,
        ),
        name="attend",
    )(*operands)

    parts = [keep, swap(send, count, stages[0][0])]
    size = half
    for stride, radix in stages[1:]:
        size //= radix
        pieces = call(
            functools.partial(merge_body, len(parts), reqs, latent),
            [spec((size, width), BF16)] * (radix - 1),
            parts,
            name="merge",
        )
        parts += [swap(pieces[j - 1], count, j * stride) for j in reversed(range(1, radix))]

    parts_out = 4
    model = out_weight.shape[1]
    quarter = model // parts_out
    keep, send = call(
        functools.partial(project_body, len(parts), reqs, heads, latent, parts_out),
        [spec((rows, 2 * quarter), F32), spec((rows, 2 * quarter), BF16)],
        parts + [value_up, out_weight],
        name="project",
    )
    kept = keep + swap(send, count, stages[0][0]).astype(F32)
    kept = kept[:, :quarter] + swap(kept[:, quarter:].astype(BF16), count, stages[1][0]).astype(F32)
    for stride, radix in stages[2:]:
        mine = kept.astype(BF16)
        terms = [mine.astype(F32)] + [
            swap(mine, count, j * stride).astype(F32) for j in range(1, radix)
        ]
        while len(terms) > 1:
            terms = [terms[i] + terms[i + 1] for i in range(0, len(terms), 2)]
        kept = terms[0]
    done = kept.astype(BF16)
    both = jnp.concatenate([done, swap(done, count, stages[1][0])], axis=1)
    other = swap(both, count, stages[0][0])
    return pl.pallas_call(
        functools.partial(place_body, parts_out),
        out_shape=spec((rows, model), BF16),
        in_specs=[pl.BlockSpec(memory_space=pltpu.VMEM)] * 2,
        out_specs=pl.BlockSpec(memory_space=pl.ANY),
        scratch_shapes=[pltpu.SemaphoreType.DMA((parts_out,))],
        compiler_params=pltpu.CompilerParams(vmem_limit_bytes=16 << 20),
        name="place",
    )(both, other)


def solution(mesh):
    placed = (
        P("groups", None),
        P(),
        P(None, "ctx"),
        P(None, "ctx"),
        P("ctx", None, None),
        P("ctx", None, None),
        P("ctx", None),
        P("groups", "ctx", None),
        P("groups", None, "ctx"),
        P("groups"),
    )
    return jax.shard_map(
        functools.partial(local, mesh.shape["ctx"]),
        mesh=mesh,
        in_specs=placed,
        out_specs=P("groups", None),
        check_vma=False,
    )
```

```python
import functools
import math

import jax
import jax.numpy as jnp
from jax import lax
from jax.experimental import pallas as pl
from jax.experimental.pallas import tpu as pltpu
from jax.sharding import PartitionSpec as P

mscale_yarn = 1.0 + 0.1 * math.log(40.0)
masked_score = -1e30
LOG2E = 1.4426950408889634
LANES = 128
F32 = jnp.float32
BF16 = jnp.bfloat16


def stage_list(count):
    stages, stride = [], 1
    while stride < count:
        left = count // stride
        radix = 2 if (stride < 4 or left < 4) else 4
        stages.append((stride, radix))
        stride *= radix
    return stages


def swap(x, count, mask):
    return lax.ppermute(x, "ctx", [(i, i ^ mask) for i in range(count)])


def call(body, outs, operands, *, flops=0, smem=(), name=None, limit=40 << 20):
    specs = [
        pl.BlockSpec(memory_space=pltpu.SMEM if i in smem else pltpu.VMEM)
        for i in range(len(operands))
    ]
    total = sum(o.size * o.dtype.itemsize for o in list(outs) + list(operands))
    return pl.pallas_call(
        body,
        out_shape=tuple(outs),
        in_specs=specs,
        out_specs=tuple(pl.BlockSpec(memory_space=pltpu.VMEM) for _ in outs),
        compiler_params=pltpu.CompilerParams(vmem_limit_bytes=limit),
        cost_estimate=pl.CostEstimate(flops=flops, bytes_accessed=total, transcendentals=0),
        name=name,
    )(*operands)


def spec(shape, dtype):
    return jax.ShapeDtypeStruct(shape, dtype)


def table_body(keys, table_ref):
    table_ref[...] = (
        lax.axis_index("ctx") * keys
        + lax.broadcasted_iota(jnp.int32, table_ref.shape, 1)
        - lax.broadcasted_iota(jnp.int32, table_ref.shape, 0)
    )


def query_body(heads, reqs, x_ref, gain_ref, nope_ref, rope_ref, key_ref, table_ref, out_ref):
    rows = x_ref.shape[0]
    stretch = rows // reqs
    nope_width, latent = key_ref.shape[1], key_ref.shape[2]
    rope_width = rope_ref.shape[1] // heads
    x = x_ref[...].astype(F32)
    mean = jnp.mean(x * x, axis=-1, keepdims=True)
    normed = (x * lax.rsqrt(mean + 1e-06) * gain_ref[...].astype(F32).reshape(1, -1)).astype(BF16)
    nope = jnp.dot(normed, nope_ref[...], preferred_element_type=F32).astype(BF16)
    rope = jnp.dot(normed, rope_ref[...], preferred_element_type=F32)
    lat = [
        jnp.dot(
            nope[:, h * nope_width : (h + 1) * nope_width], key_ref[h], preferred_element_type=F32
        )
        for h in range(heads)
    ]
    ropes = []
    for b in range(reqs):
        part = slice(b * stretch, (b + 1) * stretch)
        rows_b = jnp.concatenate([lat[h][part] for h in range(heads)], axis=0)
        out_ref[:, b * latent : (b + 1) * latent] = rows_b.astype(BF16)
        ropes.append(
            jnp.concatenate(
                [rope[part, h * rope_width : (h + 1) * rope_width] for h in range(heads)], axis=0
            )
        )
    out_ref[:, reqs * latent :] = jnp.concatenate(ropes, axis=1).astype(BF16)


def pack_stats(columns):
    rows = columns[0].shape[0]
    lane = lax.broadcasted_iota(jnp.int32, (rows, LANES), 1)
    out = jnp.zeros((rows, LANES), F32)
    for b, column in enumerate(columns):
        high = column.astype(BF16).astype(F32)
        rest = column - high
        mid = rest.astype(BF16).astype(F32)
        low = rest - mid
        for k, term in enumerate((high, mid, low)):
            out = jnp.where(lane == 3 * b + k, term, out)
    return out


def read_stats(stats, b):
    return (stats[:, 3 * b : 3 * b + 1] + stats[:, 3 * b + 1 : 3 * b + 2]) + stats[
        :, 3 * b + 2 : 3 * b + 3
    ]


def merge(parts, reqs, latent):
    tops = []
    pooled = []
    for b in range(reqs):
        lse = [read_stats(p[:, reqs * latent :], b) for p in parts]
        top = functools.reduce(jnp.maximum, lse)
        weight = [jnp.exp(m - top) for m in lse]
        total = functools.reduce(jnp.add, weight)
        inverse = 1.0 / total
        value = functools.reduce(
            jnp.add,
            [p[:, b * latent : (b + 1) * latent] * (w * inverse) for p, w in zip(parts, weight)],
        )
        pooled.append(value)
        tops.append(top + jnp.log(total))
    return pooled, tops


def attend_body(
    n_q, reqs, latent, rope_width, stretch, scale, chunk, *refs
):
    length_ref, table_ref, refs = refs[0], refs[1], refs[2:]
    q_refs = refs[:n_q]
    lat_ref, rope_ref = refs[n_q], refs[1 + n_q]
    keep_ref, send_ref = refs[2 + n_q], refs[3 + n_q]
    q_s, s_s, w_s = refs[4 + n_q :]
    rows = q_s.shape[0]
    half = rows // 2
    keys = lat_ref.shape[1]
    at = 0
    for q in q_refs:
        q_s[at : at + q.shape[0], :] = q[...]
        at += q.shape[0]
    block = min(rows, 256)
    for r0 in range(0, rows, block):
        rs = slice(r0, r0 + block)
        stats, peaks = [], []
        for b in range(reqs):
            seen = length_ref[b]
            lhs = q_s[rs, b * latent : (b + 1) * latent]
            base = reqs * latent + b * rope_width
            lhs_rope = q_s[rs, base : base + rope_width]
            peak = None
            for k0 in range(0, keys, chunk):
                s = lax.dot_general(
                    lhs,
                    lat_ref[b, k0 : k0 + chunk, :],
                    (((1,), (1,)), ((), ())),
                    preferred_element_type=F32,
                ) + jnp.dot(
                    lhs_rope, rope_ref[b, :, k0 : k0 + chunk], preferred_element_type=F32
                )
                visible = table_ref[...] + k0 <= seen
                s = jnp.where(
                    visible[None], s.reshape(block // stretch, stretch, chunk), masked_score
                ).reshape(block, chunk)
                s_s[b, :, k0 : k0 + chunk] = s
                top = jnp.max(s, axis=1, keepdims=True)
                peak = top if peak is None else jnp.maximum(peak, top)
            peaks.append(peak)
        for b in range(reqs):
            peak = peaks[b]
            total = None
            for k0 in range(0, keys, chunk):
                w = jnp.exp2((s_s[b, :, k0 : k0 + chunk] - peak) * (scale * LOG2E))
                part = jnp.sum(w, axis=1, keepdims=True)
                total = part if total is None else total + part
                w_s[b, :, k0 : k0 + chunk] = w.astype(BF16)
            pool = jnp.dot(w_s[b], lat_ref[b], preferred_element_type=F32)
            pool = pool * (1.0 / total)
            stats.append(peak * scale + jnp.log(total))
            cols = slice(b * latent, (b + 1) * latent)
            for lo in range(r0, r0 + block, min(block, half)):
                size = min(block, half)
                piece = pool[lo - r0 : lo - r0 + size]
                if lo < half:
                    keep_ref[lo : lo + size, cols] = piece
                else:
                    send_ref[lo - half : lo - half + size, cols] = piece.astype(BF16)
        packed = pack_stats(stats)
        for lo in range(r0, r0 + block, min(block, half)):
            size = min(block, half)
            piece = packed[lo - r0 : lo - r0 + size]
            if lo < half:
                keep_ref[lo : lo + size, reqs * latent :] = piece
            else:
                send_ref[lo - half : lo - half + size, reqs * latent :] = piece.astype(BF16)


def part_rows(ref, spread, place, own, lo, size):
    if not spread:
        return ref[lo : lo + size, :].astype(F32)
    blocks = [
        ref[(2 * k + place) * own : (2 * k + place + 1) * own, :]
        for k in range(lo // own, (lo + size) // own)
    ]
    return jnp.concatenate([b.astype(F32) for b in blocks], axis=0)


def merge_body(n_in, reqs, latent, own, beside, *refs):
    outs = refs[n_in:]
    size = outs[0].shape[0]
    for j, out in enumerate(outs, 1):
        lo = 0 if beside else j * size
        parts = [
            part_rows(r, i < 2, 1 if beside else 0, own, lo, size)
            for i, r in enumerate(refs[:n_in])
        ]
        pooled, tops = merge(parts, reqs, latent)
        for b in range(reqs):
            out[:, b * latent : (b + 1) * latent] = pooled[b].astype(out.dtype)
        out[:, reqs * latent :] = pack_stats(tops).astype(out.dtype)


def project_body(n_in, reqs, heads, latent, parts_out, *refs):
    own = heads * (refs[-1].shape[0] // reqs)
    parts = [r[:own, :].astype(F32) for r in refs[:n_in]]
    value_ref, weight_ref = refs[n_in], refs[n_in + 1]
    hidden_ref, send_ref = refs[n_in + 2], refs[n_in + 3]
    pooled, _ = merge(parts, reqs, latent)
    stretch = pooled[0].shape[0] // heads
    values = []
    for h in range(heads):
        rows = jnp.concatenate([p[h * stretch : (h + 1) * stretch] for p in pooled], axis=0)
        values.append(
            jnp.dot(rows.astype(BF16), value_ref[h], preferred_element_type=F32).astype(BF16)
        )
    hidden = jnp.concatenate(values, axis=1)
    hidden_ref[...] = hidden
    project_half(1, parts_out, hidden, weight_ref, send_ref)


def project_half(odd, parts_out, hidden, weight_ref, out_ref):
    mine = lax.rem(lax.axis_index("ctx"), parts_out)
    width = weight_ref.shape[1] // parts_out
    for e in range(odd, parts_out, 2):
        start = pl.multiple_of(jnp.bitwise_xor(mine, e) * width, LANES)
        out = jnp.dot(hidden, weight_ref[:, pl.ds(start, width)], preferred_element_type=F32)
        out_ref[:, (e // 2) * width : (e // 2 + 1) * width] = out.astype(out_ref.dtype)


def rest_body(parts_out, hidden_ref, weight_ref, keep_ref):
    project_half(0, parts_out, hidden_ref[...], weight_ref, keep_ref)


def join_body(*refs):
    at = 0
    for r in refs[:-1]:
        refs[-1][at : at + r.shape[0], :] = r[...]
        at += r.shape[0]


def place_body(parts_out, *refs):
    pieces, out_ref, sems = refs[:-2], refs[-2], refs[-1]
    copies = []
    mine = lax.rem(lax.axis_index("ctx"), parts_out)
    width = out_ref.shape[1] // parts_out
    e_order = (0, 2, 1, 3)
    at = 0
    for piece in pieces:
        for k in range(piece.shape[1] // width):
            start = pl.multiple_of(jnp.bitwise_xor(mine, e_order[at]) * width, LANES)
            copies.append(
                pltpu.make_async_copy(
                    piece.at[:, pl.ds(k * width, width)],
                    out_ref.at[:, pl.ds(start, width)],
                    sems.at[at],
                )
            )
            copies[-1].start()
            at += 1
    for copy in copies:
        copy.wait()


def local(count, query_input, query_gain, nope_weight, rope_weight, key_up, value_up, out_weight,
          cache_latent, cache_rope, cached_length):
    heads, nope_width, latent = key_up.shape
    reqs = cache_latent.shape[0]
    rope_width = cache_rope.shape[1]
    rows = query_input.shape[0]
    stretch = rows // reqs
    own = heads * stretch
    width = reqs * latent + LANES
    stages = stage_list(count)
    scale = mscale_yarn * mscale_yarn / math.sqrt(nope_width + rope_width)

    chunk = 256
    (table,) = call(
        functools.partial(table_body, cache_latent.shape[1]),
        [spec((stretch, chunk), jnp.int32)],
        [],
        flops=2 << 30,
        limit=16 << 20,
        name="table",
    )
    (query,) = call(
        functools.partial(query_body, heads, reqs),
        [spec((own, width), BF16)],
        [query_input, query_gain, nope_weight, rope_weight, key_up, table],
        limit=16 << 20,
        name="query",
    )
    held = jnp.concatenate([query, swap(query, count, stages[1][0])], axis=0)
    for stride, radix in reversed(stages[2:]):
        got = [swap(held, count, j * stride) for j in range(1, radix)]
        (held,) = call(
            join_body,
            [spec((radix * held.shape[0], width), BF16)],
            [held] + got,
            flops=4 << 30,
            limit=16 << 20,
            name="join",
        )
    near = held
    far = swap(near, count, stages[0][0])

    half = near.shape[0]
    total = 2 * half
    block = min(total, 256)
    operands = [cached_length, table, near, far, cache_latent, cache_rope]
    keep, send = pl.pallas_call(
        functools.partial(attend_body, 2, reqs, latent, rope_width, stretch, scale, chunk),
        out_shape=(spec((half, width), F32), spec((half, width), BF16)),
        in_specs=[pl.BlockSpec(memory_space=pltpu.SMEM)]
        + [pl.BlockSpec(memory_space=pltpu.VMEM)] * 5,
        out_specs=(pl.BlockSpec(memory_space=pltpu.VMEM),) * 2,
        scratch_shapes=[
            pltpu.VMEM((total, width), BF16),
            pltpu.VMEM((reqs, block, cache_latent.shape[1]), F32),
            pltpu.VMEM((reqs, block, cache_latent.shape[1]), BF16),
        ],
        compiler_params=pltpu.CompilerParams(vmem_limit_bytes=48 << 20),
        cost_estimate=pl.CostEstimate(
            flops=4 * total * cache_latent.shape[1] * latent * reqs,
            bytes_accessed=8 << 20,
            transcendentals=0,
        ),
        name="attend",
    )(*operands)

    parts = [keep, swap(send, count, stages[0][0])]
    size = half
    for at, (stride, radix) in enumerate(stages[1:]):
        size //= radix
        pieces = call(
            functools.partial(merge_body, len(parts), reqs, latent, own, at == 0),
            [spec((size, width), BF16)] * (radix - 1),
            parts,
            name="merge",
        )
        parts += [swap(pieces[j - 1], count, j * stride) for j in reversed(range(1, radix))]

    parts_out = 4
    model = out_weight.shape[1]
    quarter = model // parts_out
    hidden, send = call(
        functools.partial(project_body, len(parts), reqs, heads, latent, parts_out),
        [spec((rows, out_weight.shape[0]), BF16), spec((rows, 2 * quarter), BF16)],
        parts + [value_up, out_weight],
        limit=24 << 20,
        name="project",
    )
    received = swap(send, count, stages[0][0])
    (keep,) = call(
        functools.partial(rest_body, parts_out),
        [spec((rows, 2 * quarter), F32)],
        [hidden, out_weight],
        flops=2 * rows * out_weight.size // 2,
        limit=24 << 20,
        name="rest",
    )
    kept = keep + received.astype(F32)
    kept = kept[:, :quarter] + swap(kept[:, quarter:].astype(BF16), count, stages[1][0]).astype(F32)
    for stride, radix in stages[2:]:
        mine = kept.astype(BF16)
        terms = [mine.astype(F32)] + [
            swap(mine, count, j * stride).astype(F32) for j in range(1, radix)
        ]
        while len(terms) > 1:
            terms = [terms[i] + terms[i + 1] for i in range(0, len(terms), 2)]
        kept = terms[0]
    done = kept.astype(BF16)
    both = jnp.concatenate([done, swap(done, count, stages[1][0])], axis=1)
    other = swap(both, count, stages[0][0])
    return pl.pallas_call(
        functools.partial(place_body, parts_out),
        out_shape=spec((rows, model), BF16),
        in_specs=[pl.BlockSpec(memory_space=pltpu.VMEM)] * 2,
        out_specs=pl.BlockSpec(memory_space=pl.ANY),
        scratch_shapes=[pltpu.SemaphoreType.DMA((parts_out,))],
        compiler_params=pltpu.CompilerParams(vmem_limit_bytes=16 << 20),
        name="place",
    )(both, other)


def solution(mesh):
    placed = (
        P("groups", None),
        P(),
        P(None, "ctx"),
        P(None, "ctx"),
        P("ctx", None, None),
        P("ctx", None, None),
        P("ctx", None),
        P("groups", "ctx", None),
        P("groups", None, "ctx"),
        P("groups"),
    )
    return jax.shard_map(
        functools.partial(local, mesh.shape["ctx"]),
        mesh=mesh,
        in_specs=placed,
        out_specs=P("groups", None),
        check_vma=False,
    )
```

```python
import functools
import math

import jax
import jax.numpy as jnp
from jax import lax
from jax.experimental import pallas as pl
from jax.experimental.pallas import tpu as pltpu
from jax.sharding import PartitionSpec as P

mscale_yarn = 1.0 + 0.1 * math.log(40.0)
masked_score = -1e30
LOG2E = 1.4426950408889634
LANES = 128
F32 = jnp.float32
BF16 = jnp.bfloat16


def stage_list(count):
    stages, stride = [], 1
    while stride < count:
        left = count // stride
        radix = 2 if (stride < 4 or left < 4) else 4
        stages.append((stride, radix))
        stride *= radix
    return stages


def swap(x, count, mask):
    return lax.ppermute(x, "ctx", [(i, i ^ mask) for i in range(count)])


def call(body, outs, operands, *, flops=0, smem=(), name=None, limit=40 << 20):
    specs = [
        pl.BlockSpec(memory_space=pltpu.SMEM if i in smem else pltpu.VMEM)
        for i in range(len(operands))
    ]
    total = sum(o.size * o.dtype.itemsize for o in list(outs) + list(operands))
    return pl.pallas_call(
        body,
        out_shape=tuple(outs),
        in_specs=specs,
        out_specs=tuple(pl.BlockSpec(memory_space=pltpu.VMEM) for _ in outs),
        compiler_params=pltpu.CompilerParams(vmem_limit_bytes=limit),
        cost_estimate=pl.CostEstimate(flops=flops, bytes_accessed=total, transcendentals=0),
        name=name,
    )(*operands)


def spec(shape, dtype):
    return jax.ShapeDtypeStruct(shape, dtype)


def table_body(keys, table_ref):
    table_ref[...] = (
        lax.axis_index("ctx") * keys
        + lax.broadcasted_iota(jnp.int32, table_ref.shape, 1)
        - lax.broadcasted_iota(jnp.int32, table_ref.shape, 0)
    )


def query_body(heads, reqs, x_ref, gain_ref, nope_ref, rope_ref, key_ref, table_ref, out_ref):
    rows = x_ref.shape[0]
    stretch = rows // reqs
    nope_width, latent = key_ref.shape[1], key_ref.shape[2]
    rope_width = rope_ref.shape[1] // heads
    x = x_ref[...].astype(F32)
    mean = jnp.mean(x * x, axis=-1, keepdims=True)
    normed = (x * lax.rsqrt(mean + 1e-06) * gain_ref[...].astype(F32).reshape(1, -1)).astype(BF16)
    nope = jnp.dot(normed, nope_ref[...], preferred_element_type=F32).astype(BF16)
    rope = jnp.dot(normed, rope_ref[...], preferred_element_type=F32)
    lat = [
        jnp.dot(
            nope[:, h * nope_width : (h + 1) * nope_width], key_ref[h], preferred_element_type=F32
        )
        for h in range(heads)
    ]
    ropes = []
    for b in range(reqs):
        part = slice(b * stretch, (b + 1) * stretch)
        rows_b = jnp.concatenate([lat[h][part] for h in range(heads)], axis=0)
        out_ref[:, b * latent : (b + 1) * latent] = rows_b.astype(BF16)
        ropes.append(
            jnp.concatenate(
                [rope[part, h * rope_width : (h + 1) * rope_width] for h in range(heads)], axis=0
            )
        )
    out_ref[:, reqs * latent :] = jnp.concatenate(ropes, axis=1).astype(BF16)


def pack_stats(columns):
    rows = columns[0].shape[0]
    lane = lax.broadcasted_iota(jnp.int32, (rows, LANES), 1)
    out = jnp.zeros((rows, LANES), F32)
    for b, column in enumerate(columns):
        high = column.astype(BF16).astype(F32)
        rest = column - high
        mid = rest.astype(BF16).astype(F32)
        low = rest - mid
        for k, term in enumerate((high, mid, low)):
            out = jnp.where(lane == 3 * b + k, term, out)
    return out


def read_stats(stats, b):
    return (stats[:, 3 * b : 3 * b + 1] + stats[:, 3 * b + 1 : 3 * b + 2]) + stats[
        :, 3 * b + 2 : 3 * b + 3
    ]


def merge(parts, reqs, latent):
    tops = []
    pooled = []
    for b in range(reqs):
        lse = [read_stats(p[:, reqs * latent :], b) for p in parts]
        top = functools.reduce(jnp.maximum, lse)
        weight = [jnp.exp(m - top) for m in lse]
        total = functools.reduce(jnp.add, weight)
        inverse = 1.0 / total
        value = functools.reduce(
            jnp.add,
            [p[:, b * latent : (b + 1) * latent] * (w * inverse) for p, w in zip(parts, weight)],
        )
        pooled.append(value)
        tops.append(top + jnp.log(total))
    return pooled, tops


def attend_body(
    n_q, reqs, latent, rope_width, stretch, scale, chunk, *refs
):
    length_ref, table_ref, refs = refs[0], refs[1], refs[2:]
    q_refs = refs[:n_q]
    lat_ref, rope_ref = refs[n_q], refs[1 + n_q]
    keep_ref, send_ref = refs[2 + n_q], refs[3 + n_q]
    q_s, s_s, w_s = refs[4 + n_q :]
    rows = q_s.shape[0]
    half = rows // 2
    keys = lat_ref.shape[1]
    at = 0
    for q in q_refs:
        q_s[at : at + q.shape[0], :] = q[...]
        at += q.shape[0]
    block = min(rows, 256)
    for r0 in range(0, rows, block):
        rs = slice(r0, r0 + block)
        stats, peaks = [], []
        for b in range(reqs):
            seen = length_ref[b]
            lhs = q_s[rs, b * latent : (b + 1) * latent]
            base = reqs * latent + b * rope_width
            lhs_rope = q_s[rs, base : base + rope_width]
            peak = None
            for k0 in range(0, keys, chunk):
                s = lax.dot_general(
                    lhs,
                    lat_ref[b, k0 : k0 + chunk, :],
                    (((1,), (1,)), ((), ())),
                    preferred_element_type=F32,
                ) + jnp.dot(
                    lhs_rope, rope_ref[b, :, k0 : k0 + chunk], preferred_element_type=F32
                )
                visible = table_ref[...] + k0 <= seen
                s = jnp.where(
                    visible[None], s.reshape(block // stretch, stretch, chunk), masked_score
                ).reshape(block, chunk)
                s_s[b, :, k0 : k0 + chunk] = s
                top = jnp.max(s, axis=1, keepdims=True)
                peak = top if peak is None else jnp.maximum(peak, top)
            peaks.append(peak)
        for b in range(reqs):
            peak = peaks[b]
            total = None
            for k0 in range(0, keys, chunk):
                w = jnp.exp2((s_s[b, :, k0 : k0 + chunk] - peak) * (scale * LOG2E))
                part = jnp.sum(w, axis=1, keepdims=True)
                total = part if total is None else total + part
                w_s[b, :, k0 : k0 + chunk] = w.astype(BF16)
            pool = jnp.dot(w_s[b], lat_ref[b], preferred_element_type=F32)
            pool = pool * (1.0 / total)
            stats.append(peak * scale + jnp.log(total))
            cols = slice(b * latent, (b + 1) * latent)
            for lo in range(r0, r0 + block, min(block, half)):
                size = min(block, half)
                piece = pool[lo - r0 : lo - r0 + size]
                if lo < half:
                    keep_ref[lo : lo + size, cols] = piece
                else:
                    send_ref[lo - half : lo - half + size, cols] = piece.astype(BF16)
        packed = pack_stats(stats)
        for lo in range(r0, r0 + block, min(block, half)):
            size = min(block, half)
            piece = packed[lo - r0 : lo - r0 + size]
            if lo < half:
                keep_ref[lo : lo + size, reqs * latent :] = piece
            else:
                send_ref[lo - half : lo - half + size, reqs * latent :] = piece.astype(BF16)


def part_rows(ref, spread, place, own, lo, size):
    if not spread:
        return ref[lo : lo + size, :].astype(F32)
    blocks = [
        ref[(2 * k + place) * own : (2 * k + place + 1) * own, :]
        for k in range(lo // own, (lo + size) // own)
    ]
    return jnp.concatenate([b.astype(F32) for b in blocks], axis=0)


def merge_body(n_in, reqs, latent, own, beside, *refs):
    outs = refs[n_in:]
    size = outs[0].shape[0]
    for j, out in enumerate(outs, 1):
        lo = 0 if beside else j * size
        parts = [
            part_rows(r, i < 2, 1 if beside else 0, own, lo, size)
            for i, r in enumerate(refs[:n_in])
        ]
        pooled, tops = merge(parts, reqs, latent)
        for b in range(reqs):
            out[:, b * latent : (b + 1) * latent] = pooled[b].astype(out.dtype)
        out[:, reqs * latent :] = pack_stats(tops).astype(out.dtype)


def project_body(n_in, reqs, heads, latent, parts_out, *refs):
    own = heads * (refs[-1].shape[0] // reqs)
    parts = [r[:own, :].astype(F32) for r in refs[:n_in]]
    value_ref, weight_ref = refs[n_in], refs[n_in + 1]
    hidden_ref, send_ref = refs[n_in + 2], refs[n_in + 3]
    pooled, _ = merge(parts, reqs, latent)
    stretch = pooled[0].shape[0] // heads
    values = []
    for h in range(heads):
        rows = jnp.concatenate([p[h * stretch : (h + 1) * stretch] for p in pooled], axis=0)
        values.append(
            jnp.dot(rows.astype(BF16), value_ref[h], preferred_element_type=F32).astype(BF16)
        )
    hidden = jnp.concatenate(values, axis=1)
    hidden_ref[...] = hidden
    project_half(1, parts_out, hidden, weight_ref, send_ref)


def project_half(odd, parts_out, hidden, weight_ref, out_ref):
    mine = lax.rem(lax.axis_index("ctx"), parts_out)
    width = weight_ref.shape[1] // parts_out
    for e in range(odd, parts_out, 2):
        start = pl.multiple_of(jnp.bitwise_xor(mine, e) * width, LANES)
        out = jnp.dot(hidden, weight_ref[:, pl.ds(start, width)], preferred_element_type=F32)
        out_ref[:, (e // 2) * width : (e // 2 + 1) * width] = out.astype(out_ref.dtype)


def rest_body(parts_out, hidden_ref, weight_ref, keep_ref):
    project_half(0, parts_out, hidden_ref[...], weight_ref, keep_ref)


def join_body(*refs):
    at = 0
    for r in refs[:-1]:
        refs[-1][at : at + r.shape[0], :] = r[...]
        at += r.shape[0]


def place_body(parts_out, order, piece, *refs):
    out_ref, sems = refs[-2:]
    mine = lax.rem(lax.axis_index("ctx"), parts_out)
    width = out_ref.shape[1] // parts_out
    copies = []
    for k, e in enumerate(order):
        start = pl.multiple_of(jnp.bitwise_xor(mine, e) * width, LANES)
        copies.append(
            pltpu.make_async_copy(
                piece.at[:, pl.ds(k * width, width)],
                out_ref.at[:, pl.ds(start, width)],
                sems.at[k],
            )
        )
        copies[-1].start()
    for copy in copies:
        copy.wait()


def place(parts_out, order, piece, shape, into=()):
    return pl.pallas_call(
        functools.partial(place_body, parts_out, order),
        out_shape=shape,
        in_specs=[pl.BlockSpec(memory_space=pltpu.VMEM)]
        + [pl.BlockSpec(memory_space=pl.ANY)] * len(into),
        out_specs=pl.BlockSpec(memory_space=pl.ANY),
        scratch_shapes=[pltpu.SemaphoreType.DMA((len(order),))],
        input_output_aliases={1: 0} if into else {},
        compiler_params=pltpu.CompilerParams(vmem_limit_bytes=16 << 20),
        cost_estimate=pl.CostEstimate(
            flops=0, bytes_accessed=2 * piece.size * 2, transcendentals=0
        ),
        name="place",
    )(piece, *into)


def local(count, query_input, query_gain, nope_weight, rope_weight, key_up, value_up, out_weight,
          cache_latent, cache_rope, cached_length):
    heads, nope_width, latent = key_up.shape
    reqs = cache_latent.shape[0]
    rope_width = cache_rope.shape[1]
    rows = query_input.shape[0]
    stretch = rows // reqs
    own = heads * stretch
    width = reqs * latent + LANES
    stages = stage_list(count)
    scale = mscale_yarn * mscale_yarn / math.sqrt(nope_width + rope_width)

    chunk = 256
    (table,) = call(
        functools.partial(table_body, cache_latent.shape[1]),
        [spec((stretch, chunk), jnp.int32)],
        [],
        flops=2 << 30,
        limit=16 << 20,
        name="table",
    )
    (query,) = call(
        functools.partial(query_body, heads, reqs),
        [spec((own, width), BF16)],
        [query_input, query_gain, nope_weight, rope_weight, key_up, table],
        limit=16 << 20,
        name="query",
    )
    held = jnp.concatenate([query, swap(query, count, stages[1][0])], axis=0)
    for stride, radix in reversed(stages[2:]):
        got = [swap(held, count, j * stride) for j in range(1, radix)]
        (held,) = call(
            join_body,
            [spec((radix * held.shape[0], width), BF16)],
            [held] + got,
            flops=4 << 30,
            limit=16 << 20,
            name="join",
        )
    near = held
    far = swap(near, count, stages[0][0])

    half = near.shape[0]
    total = 2 * half
    block = min(total, 256)
    operands = [cached_length, table, near, far, cache_latent, cache_rope]
    keep, send = pl.pallas_call(
        functools.partial(attend_body, 2, reqs, latent, rope_width, stretch, scale, chunk),
        out_shape=(spec((half, width), F32), spec((half, width), BF16)),
        in_specs=[pl.BlockSpec(memory_space=pltpu.SMEM)]
        + [pl.BlockSpec(memory_space=pltpu.VMEM)] * 5,
        out_specs=(pl.BlockSpec(memory_space=pltpu.VMEM),) * 2,
        scratch_shapes=[
            pltpu.VMEM((total, width), BF16),
            pltpu.VMEM((reqs, block, cache_latent.shape[1]), F32),
            pltpu.VMEM((reqs, block, cache_latent.shape[1]), BF16),
        ],
        compiler_params=pltpu.CompilerParams(vmem_limit_bytes=48 << 20),
        cost_estimate=pl.CostEstimate(
            flops=4 * total * cache_latent.shape[1] * latent * reqs,
            bytes_accessed=8 << 20,
            transcendentals=0,
        ),
        name="attend",
    )(*operands)

    parts = [keep, swap(send, count, stages[0][0])]
    size = half
    for at, (stride, radix) in enumerate(stages[1:]):
        size //= radix
        pieces = call(
            functools.partial(merge_body, len(parts), reqs, latent, own, at == 0),
            [spec((size, width), BF16)] * (radix - 1),
            parts,
            name="merge",
        )
        parts += [swap(pieces[j - 1], count, j * stride) for j in reversed(range(1, radix))]

    parts_out = 4
    model = out_weight.shape[1]
    quarter = model // parts_out
    hidden, send = call(
        functools.partial(project_body, len(parts), reqs, heads, latent, parts_out),
        [spec((rows, out_weight.shape[0]), BF16), spec((rows, 2 * quarter), BF16)],
        parts + [value_up, out_weight],
        limit=24 << 20,
        name="project",
    )
    received = swap(send, count, stages[0][0])
    (keep,) = call(
        functools.partial(rest_body, parts_out),
        [spec((rows, 2 * quarter), F32)],
        [hidden, out_weight],
        flops=2 * rows * out_weight.size // 2,
        limit=24 << 20,
        name="rest",
    )
    kept = keep + received.astype(F32)
    kept = kept[:, :quarter] + swap(kept[:, quarter:].astype(BF16), count, stages[1][0]).astype(F32)
    for stride, radix in stages[2:]:
        mine = kept.astype(BF16)
        terms = [mine.astype(F32)] + [
            swap(mine, count, j * stride).astype(F32) for j in range(1, radix)
        ]
        while len(terms) > 1:
            terms = [terms[i] + terms[i + 1] for i in range(0, len(terms), 2)]
        kept = terms[0]
    done = kept.astype(BF16)
    both = jnp.concatenate([done, swap(done, count, stages[1][0])], axis=1)
    other = swap(both, count, stages[0][0])
    shape = spec((rows, model), BF16)
    first = place(parts_out, (0, 2), both, shape)
    return place(parts_out, (1, 3), other, shape, (first,))


def solution(mesh):
    placed = (
        P("groups", None),
        P(),
        P(None, "ctx"),
        P(None, "ctx"),
        P("ctx", None, None),
        P("ctx", None, None),
        P("ctx", None),
        P("groups", "ctx", None),
        P("groups", None, "ctx"),
        P("groups"),
    )
    return jax.shard_map(
        functools.partial(local, mesh.shape["ctx"]),
        mesh=mesh,
        in_specs=placed,
        out_specs=P("groups", None),
        check_vma=False,
    )
```
